768 devices in a mesh: dom: 96 (over x, z, core), feat: 8 (over y).
Axes of the slice: x: 4, y: 8, z: 12, core: 2. Of those that a mesh axis runs over, the one named last changes fastest.
Arguments:
- features: bfloat16 [49152, 256], P('dom', 'feat'), may hold values from -6 to 6
- weight: bfloat16 [512, 256], P(None, 'feat'), may hold values from -0.25 to 0.25
- bias: bfloat16 [256], P('feat'), may hold values from -3 to 3
- local_src: int32 [196608], P('dom'), may hold values from 0 to 511
- local_dst: int32 [196608], P('dom'), may hold values from 0 to 511
- hub_rows: int32 [1536], P('dom'), may hold values from 0 to 511
- hub_src: int32 [98304], P('dom'), may hold values from 0 to 1535
- hub_dst: int32 [98304], P('dom'), may hold values from 0 to 511
- send_rows: int32 [9216, 8], P('dom'), may hold values from 0 to 511
- bnd_src: int32 [98304], P('dom'), may hold values from 0 to 767
- bnd_dst: int32 [98304], P('dom'), may hold values from 0 to 511
Outputs:
- hidden: bfloat16 [49152, 256], P('dom', 'feat')
The draws below stay inside these ranges and needn't reach their ends.
All inputs are finite; a program needn't handle non-finite values.
Results may differ from the reference program's by a relative error of at most 0.0027.
Values may be sent and summed in bfloat16 or wider, within the bound.
A program may use at most 32 MiB of HBM per device.

```python
import math
import jax
import jax.numpy as jnp
import numpy as np
from jax import lax

F = 256
NODE_DEV = 512
HUB_DEV = 16
CAP = 8
LE_DEV = 2048
HE_DEV = 1024
BE_DEV = 1024
NODES = 49152
HUBS = 1536
N_DOM = 96


def set_ends(drawn, own_key, least, largest):
    dims = drawn.shape
    place = [jax.random.randint(jax.random.fold_in(own_key, axis), (), 0, dims[axis]) for axis in range(len(dims))]
    drawn = drawn.at[tuple(place)].set(least)
    longest = dims.index(max(dims))
    place[longest] = (place[longest] + 1) % dims[longest]
    return drawn.at[tuple(place)].set(largest)


def level_of(stream_key, extent, shards, low, high):
    factor_of = 1.0
    for axis_at, shards_of in shards:
        heights = jax.random.uniform(jax.random.fold_in(jax.random.fold_in(stream_key, 6), axis_at), (shards_of,), jnp.float32, low / len(shards), high / len(shards))
        factor_of = factor_of * jnp.repeat(jnp.exp(heights), extent[axis_at] // shards_of).reshape((-1,) + (1,) * (len(extent) - 1 - axis_at))
    return factor_of


def cumulative_ranks(amount, skew):
    portions = [(1 << 20) // math.isqrt(rank ** skew) + 1 for rank in range(1, amount + 1)]
    width = 1 + sum(portions) // (1 << 30)
    return np.cumsum(np.array([max(1, weight // width) for weight in portions]))


def ranked(key, dims, number_of, lean):
    grid = cumulative_ranks(number_of, lean)
    pick = jax.random.randint(jax.random.fold_in(key, 1), dims, 0, int(grid[number_of - 1]))
    standing = jnp.searchsorted(jnp.asarray(grid, jnp.int32), pick, side="right")
    return jax.random.permutation(jax.random.fold_in(key, 2), number_of)[standing].astype(jnp.int32)


def bell_draw(stream_key, dims, width, reach, split=(), dtype=jnp.bfloat16):
    loudness = level_of(stream_key, dims, split, -0.22, 0.18) if split else 1.0
    drawn = jax.random.normal(stream_key, dims, jnp.float32) * width * loudness
    return jnp.minimum(jnp.maximum(drawn, -reach), reach).astype(dtype)


def setup_inputs(seed: int = 0) -> dict:
    seeds = jax.random.split(jax.random.key(seed), 12)
    return {
        "features": bell_draw(seeds[0], (NODES, F), 1.0, 6.0, ((0, 96), (1, 8))),
        "weight": bell_draw(seeds[1], (2 * F, F), (2 * F) ** -0.5, 0.25, ((1, 8),)),
        "bias": bell_draw(seeds[2], (F,), 0.5, 3.0, ((0, 8),)),
        "local_src": set_ends(jax.random.randint(seeds[3], (N_DOM * LE_DEV,), 0, NODE_DEV), jax.random.fold_in(seeds[3], 1), 0, NODE_DEV - 1).astype(jnp.int32),
        "local_dst": set_ends(ranked(seeds[4], (N_DOM * LE_DEV,), NODE_DEV, 2), jax.random.fold_in(seeds[4], 3), 0, NODE_DEV - 1).astype(jnp.int32),
        "hub_rows": set_ends(jax.random.randint(seeds[5], (HUBS,), 0, NODE_DEV), jax.random.fold_in(seeds[5], 1), 0, NODE_DEV - 1).astype(jnp.int32),
        "hub_src": set_ends(ranked(seeds[6], (N_DOM * HE_DEV,), HUBS, 1), jax.random.fold_in(seeds[6], 3), 0, HUBS - 1).astype(jnp.int32),
        "hub_dst": set_ends(ranked(seeds[7], (N_DOM * HE_DEV,), NODE_DEV, 2), jax.random.fold_in(seeds[7], 3), 0, NODE_DEV - 1).astype(jnp.int32),
        "send_rows": set_ends(jax.random.randint(seeds[8], (N_DOM * N_DOM, CAP), 0, NODE_DEV), jax.random.fold_in(seeds[8], 1), 0, NODE_DEV - 1).astype(jnp.int32),
        "bnd_src": set_ends(jax.random.randint(seeds[9], (N_DOM * BE_DEV,), 0, N_DOM * CAP), jax.random.fold_in(seeds[9], 1), 0, (N_DOM * CAP) - 1).astype(jnp.int32),
        "bnd_dst": set_ends(ranked(seeds[10], (N_DOM * BE_DEV,), NODE_DEV, 2), jax.random.fold_in(seeds[10], 3), 0, NODE_DEV - 1).astype(jnp.int32),
    }


def reference(features, weight, bias, local_src, local_dst, hub_rows, hub_src, hub_dst, send_rows, bnd_src, bnd_dst):
    blocks = features.reshape(N_DOM, NODE_DEV, F)
    hub_idx = hub_rows.reshape(N_DOM, HUB_DEV)
    hub_table = jax.vmap(lambda rows, idx: jnp.take(rows, idx, axis=0))(blocks, hub_idx).reshape(HUBS, F)
    send_idx = send_rows.reshape(N_DOM, N_DOM, CAP)
    outgoing = jax.vmap(lambda rows, idx: jnp.take(rows, idx, axis=0))(blocks, send_idx)
    incoming_all = jnp.transpose(outgoing, (1, 0, 2, 3)).reshape(N_DOM, N_DOM * CAP, F)

    def one_part(args):
        rows, received, lsrc, ldst, hsrc, hdst, bsrc, bdst = args
        pooled = jax.ops.segment_sum(jnp.take(rows, lsrc, axis=0).astype(jnp.float32), ldst, num_segments=NODE_DEV)
        pooled = pooled + jax.ops.segment_sum(jnp.take(hub_table, hsrc, axis=0).astype(jnp.float32), hdst, num_segments=NODE_DEV)
        pooled = pooled + jax.ops.segment_sum(jnp.take(received, bsrc, axis=0).astype(jnp.float32), bdst, num_segments=NODE_DEV)
        degree = jax.ops.segment_sum(jnp.ones(ldst.shape, jnp.float32), ldst, num_segments=NODE_DEV)
        degree = degree + jax.ops.segment_sum(jnp.ones(hdst.shape, jnp.float32), hdst, num_segments=NODE_DEV)
        degree = degree + jax.ops.segment_sum(jnp.ones(bdst.shape, jnp.float32), bdst, num_segments=NODE_DEV)
        mean_rows = (pooled / jnp.maximum(degree, 1.0)[:, None]).astype(jnp.bfloat16)
        out = jnp.dot(rows, weight[:F], preferred_element_type=jnp.float32)
        out = out + jnp.dot(mean_rows, weight[F:], preferred_element_type=jnp.float32)
        out = out + bias.astype(jnp.float32)[None, :]
        return jnp.maximum(out, 0.0).astype(jnp.bfloat16)

    result = lax.map(one_part, (blocks, incoming_all,
                                local_src.reshape(N_DOM, LE_DEV), local_dst.reshape(N_DOM, LE_DEV),
                                hub_src.reshape(N_DOM, HE_DEV), hub_dst.reshape(N_DOM, HE_DEV),
                                bnd_src.reshape(N_DOM, BE_DEV), bnd_dst.reshape(N_DOM, BE_DEV)))
    return result.reshape(NODES, F)
```

```python
import jax
import jax.numpy as jnp
from jax import lax
from jax.experimental import pallas as pl
from jax.experimental.pallas import tpu as pltpu
from jax.sharding import PartitionSpec as P

MESH = pl.DeviceIdType.MESH
BF = jnp.bfloat16
F32 = jnp.float32
NX, NZ, NY = 4, 12, 8
NQ = NX * NZ
NODES = 512
W = 32
ROWS = NQ * 8
HALF = 4 * ROWS
EDGES = 2048


def dist(step, size):
    return min(step, size - step)


OFFSETS = sorted(
    [(dx, dz) for dx in range(NX) for dz in range(NZ) if (dx, dz) != (0, 0)],
    key=lambda o: -(dist(o[0], NX) + dist(o[1], NZ)),
)
Y_ORDER = (4, 3, 5, 2, 6, 1, 7)


def nt(a, b):
    return lax.dot_general(a, b, (((1,), (1,)), ((), ())), preferred_element_type=F32)


def nn(a, b):
    return jnp.dot(a, b, preferred_element_type=F32)


def one_hot(row, size):
    at = lax.broadcasted_iota(jnp.int32, (size, row.shape[1]), 0)
    return jnp.where(at == row, 1.0, 0.0).astype(BF)


def kernel(
    x_hbm, w_hbm, b_hbm, ls_hbm, ld_hbm, hr_hbm, hs_hbm, hd_hbm, sr_hbm, bs_hbm, bd_hbm,
    o_ref,
    w_v, b_v, ls_v, ld_v, hr_v, es_v, ed_v, sr_v, xg, ot, ld1, ls1, ed1, es1, al, ar, pick,
    sendb, recv, in_sem, y_send, y_recv, d_send, d_recv, c_send, c_recv,
):
    dom, f = lax.axis_index("dom"), lax.axis_index("feat")
    core = dom % 2
    q = dom // 2
    z, x = q % NZ, q // NZ

    def chip(dx, dz):
        return lax.rem(x + dx, NX) * NZ + lax.rem(z + dz, NZ)

    sibling = q * 2 + (1 - core)
    barrier = pltpu.get_barrier_semaphore()
    for dx, dz in OFFSETS:
        pl.semaphore_signal(
            barrier, inc=1, device_id={"dom": chip(dx, dz) * 2 + core}, device_id_type=MESH
        )
    for i in Y_ORDER:
        pl.semaphore_signal(
            barrier, inc=1, device_id={"feat": lax.rem(f + i, NY)}, device_id_type=MESH
        )
    pl.semaphore_signal(barrier, inc=1, device_id={"dom": sibling}, device_id_type=MESH)

    loads = []
    for n, (src, dst) in enumerate((
        (x_hbm, xg.at[f]), (sr_hbm, sr_v), (hr_hbm, hr_v), (w_hbm, w_v), (b_hbm, b_v),
        (ls_hbm, ls_v), (ld_hbm, ld_v),
        (hs_hbm, es_v.at[pl.ds(0, 8)]), (bs_hbm, es_v.at[pl.ds(8, 8)]),
        (hd_hbm, ed_v.at[pl.ds(0, 8)]), (bd_hbm, ed_v.at[pl.ds(8, 8)]),
    )):
        copy = pltpu.make_async_copy(src, dst, in_sem.at[n])
        copy.start()
        loads.append(copy)
    for copy in loads:
        copy.wait()

    def send_lists():
        lane = lax.broadcasted_iota(jnp.int32, (16, 512), 1)
        hub = lax.broadcasted_iota(jnp.int32, (16, 512), 0)
        spread = jnp.where(
            (lane // 128 == hub % 4) & (lane % 128 == 96 + hub // 4), 1.0, 0.0
        ).astype(BF)
        hub_lanes = nn(one_hot(hr_v[...], NODES), spread)
        for c in range(8):
            part = one_hot(sr_v[c : c + 1, :], NODES)
            part = jnp.concatenate([part, jnp.zeros((NODES, 32), BF)], axis=1)
            j, si = c % 4, c // 4
            if si == 0:
                part = part + hub_lanes[:, j * 128 : j * 128 + 128].astype(BF)
            ot[:, j * 256 + si * 128 : j * 256 + si * 128 + 128] = part
        row = lax.broadcasted_iota(jnp.int32, (ROWS, 256), 0)
        col = lax.broadcasted_iota(jnp.int32, (ROWS, 256), 1)
        t = row % 8
        want = jnp.where(t < 4, (t % 2) * 128 + (row // 8) * 2 + t // 2, 92 + t)
        pick[...] = jnp.where(col == want, 1.0, 0.0).astype(BF)

    def hot_rows(ref, at, out, size):
        @pl.loop(0, EDGES // 128)
        def _(i):
            lanes = pl.ds(pl.multiple_of(i * 128, 128), 128)
            out[0:size, lanes] = one_hot(ref[pl.ds(i, 1), :] - at, size)

    send_lists()
    pl.semaphore_wait(barrier, len(OFFSETS) + NY)

    sends = []
    for i in Y_ORDER:
        copy = pltpu.make_async_remote_copy(
            src_ref=xg.at[f], dst_ref=xg.at[f], send_sem=y_send, recv_sem=y_recv,
            device_id={"feat": lax.rem(f + i, NY)}, device_id_type=MESH,
        )
        copy.start()

    ls1[NODES : NODES + 16, :] = jnp.ones((16, EDGES), BF)
    es1[ROWS : ROWS + 16, :] = jnp.ones((16, EDGES), BF)
    hot_rows(ls_v, 0, ls1, NODES)
    hot_rows(ld_v, 0, ld1, NODES)
    hot_rows(ed_v, 0, ed1, NODES)
    counts = nt(ls1[...], ld1[...])
    al[...] = counts[:NODES].astype(BF)
    degree = counts[NODES : NODES + 1]

    h = es_v[0:8, :]
    s = h // 16
    es_v[0:8, :] = (s % 2) * HALF + (h % 4) * ROWS + (s // 2) * 8 + 4 + (h // 4) % 4
    b = es_v[8:16, :]
    s = b // 8
    es_v[8:16, :] = (s % 2) * HALF + (b % 4) * ROWS + (s // 2) * 8 + 2 * core + (b // 4) % 2

    def count_block(k):
        hot_rows(es_v, k * ROWS, es1, ROWS)
        got = nt(es1[...], ed1[...])
        ar[pl.ds(pl.multiple_of(k * ROWS, 16), ROWS), :] = got[:ROWS].astype(BF)
        return got[ROWS : ROWS + 1]

    degree = degree + count_block(0)

    @pl.loop(1, 4)
    def _(k):
        count_block(k)

    all_y = pltpu.make_async_copy(xg.at[pl.ds(0, 7)], xg.at[pl.ds(0, 7)], y_recv)
    all_y.wait()

    both = jnp.concatenate([w_v[:, 256:512], w_v[:, 0:256]], axis=0)
    yz = nn(both, xg[...].reshape(NY * W, NODES))
    high = yz[0:W].astype(BF)
    low = (yz[0:W] - high.astype(F32)).astype(BF)
    lists = jnp.concatenate(
        [nn(high, ot[:, j * 256 : j * 256 + 256]) for j in range(4)], axis=0
    ).astype(BF)
    sendb[...] = nt(pick[...], lists).reshape(NQ, 8, 128).astype(BF)

    for dx, dz in OFFSETS:
        to = chip(dx, dz)
        copy = pltpu.make_async_remote_copy(
            src_ref=sendb.at[to], dst_ref=recv.at[core, q], send_sem=d_send, recv_sem=d_recv,
            device_id={"dom": to * 2 + core}, device_id_type=MESH,
        )
        copy.start()
    recv[core, q] = sendb[q]

    @pl.loop(4, 8)
    def _(k):
        count_block(k)

    near = nn(jnp.concatenate([high, low], axis=0), al[...])
    pooled = near[0:W] + near[W : 2 * W]
    diag = lax.broadcasted_iota(jnp.int32, (W, W), 0) == lax.broadcasted_iota(jnp.int32, (W, W), 1)
    bias = jnp.sum(jnp.where(diag, b_v[...].astype(F32), 0.0), axis=1, keepdims=True)
    eye = jnp.where(
        lax.broadcasted_iota(jnp.int32, (128, 128), 0)
        == lax.broadcasted_iota(jnp.int32, (128, 128), 1), 1.0, 0.0,
    ).astype(BF)

    def add_half(side):
        rows = recv[side].reshape(ROWS, 128)
        turned = nt(eye, rows).astype(BF)
        wide = jnp.concatenate([turned[j * W : j * W + W] for j in range(4)], axis=1)
        return nn(wide, ar[pl.ds(pl.multiple_of(side * HALF, 16), HALF), :])

    all_d = pltpu.make_async_copy(recv.at[0, pl.ds(0, NQ - 1)], recv.at[0, pl.ds(0, NQ - 1)], d_recv)
    all_d.wait()
    swap = pltpu.make_async_remote_copy(
        src_ref=recv.at[core], dst_ref=recv.at[core], send_sem=c_send, recv_sem=c_recv,
        device_id={"dom": sibling}, device_id_type=MESH,
    )
    swap.start()
    pooled = pooled + add_half(core)
    swap.wait_recv()
    pooled = pooled + add_half(1 - core)

    out = yz[W : 2 * W] + bias + pooled / jnp.maximum(degree, 1.0)
    o_ref[...] = jnp.maximum(out, 0.0).astype(BF)
    pltpu.make_async_copy(xg.at[pl.ds(0, 7)], xg.at[pl.ds(0, 7)], y_send).wait()
    pltpu.make_async_copy(
        recv.at[0, pl.ds(0, NQ - 1)], recv.at[0, pl.ds(0, NQ - 1)], d_send
    ).wait()
    swap.wait_send()


def shards(
    features, weight, bias, local_src, local_dst, hub_rows, hub_src, hub_dst, send_rows,
    bnd_src, bnd_dst,
):
    V = pltpu.VMEM
    I32 = jnp.int32
    DMA = pltpu.SemaphoreType.DMA
    out = pl.pallas_call(
        kernel,
        out_shape=jax.ShapeDtypeStruct((W, NODES), BF),
        in_specs=[pl.BlockSpec(memory_space=pl.ANY)] * 11,
        out_specs=pl.BlockSpec(memory_space=pltpu.VMEM),
        scratch_shapes=[
            V((W, NODES), BF), V((1, W), BF), V((16, 128), I32), V((16, 128), I32),
            V((1, 16), I32), V((16, 128), I32), V((16, 128), I32), V((8, 96), I32),
            V((NY, W, NODES), BF), V((NODES, 1024), BF),
            V((NODES, EDGES), BF), V((NODES + 16, EDGES), BF),
            V((NODES, EDGES), BF), V((ROWS + 16, EDGES), BF),
            V((NODES, NODES), BF), V((2 * HALF, NODES), BF), V((ROWS, 256), BF),
            V((NQ, 8, 128), BF), V((2, NQ, 8, 128), BF),
            DMA((11,)), DMA(()), DMA(()), DMA(()), DMA(()), DMA(()), DMA(()),
        ],
        compiler_params=pltpu.CompilerParams(
            collective_id=0, has_side_effects=True, vmem_limit_bytes=56 * 1024 * 1024
        ),
    )(
        features.T, weight.T, bias.reshape(1, W),
        local_src.reshape(16, 128), local_dst.reshape(16, 128), hub_rows.reshape(1, 16),
        hub_src.reshape(8, 128), hub_dst.reshape(8, 128), send_rows.T,
        bnd_src.reshape(8, 128), bnd_dst.reshape(8, 128),
    )
    return out.T


def solution(mesh):
    return jax.shard_map(
        shards,
        mesh=mesh,
        in_specs=(
            P("dom", "feat"), P(None, "feat"), P("feat"), P("dom"), P("dom"), P("dom"),
            P("dom"), P("dom"), P("dom", None), P("dom"), P("dom"),
        ),
        out_specs=P("dom", "feat"),
        check_vma=False,
    )
```

```python
import jax
import jax.numpy as jnp
from jax import lax
from jax.experimental import pallas as pl
from jax.experimental.pallas import tpu as pltpu
from jax.sharding import PartitionSpec as P

MESH = pl.DeviceIdType.MESH
BF = jnp.bfloat16
F32 = jnp.float32
NX, NZ, NY = 4, 12, 8
NG = NX * 2
NODES = 512
W = 32
EDGES = 2048
SPAN = 4
PART = SPAN * NG * 8
PARTS = NZ // SPAN
Y_ORDER = (4, 3, 5, 2, 6, 1, 7)


def nt(a, b):
    return lax.dot_general(a, b, (((1,), (1,)), ((), ())), preferred_element_type=F32)


def nn(a, b):
    return jnp.dot(a, b, preferred_element_type=F32)


def one_hot(row, size):
    at = lax.broadcasted_iota(jnp.int32, (size, row.shape[1]), 0)
    return jnp.where(at == row, 1.0, 0.0).astype(BF)


def kernel(
    x_hbm, w_hbm, b_hbm, ls_hbm, ld_hbm, hr_hbm, hs_hbm, hd_hbm, sr_hbm, bs_hbm, bd_hbm,
    o_ref,
    w_v, b_v, ls_v, ld_v, hr_v, es_v, ed_v, sr_v, xg, ng, ot, ld1, ls1, ed1, es1, al, ar, pick,
    sendb, recv, in_sem, ready, x_send, x_recv, n_send, n_recv, d_send, d_recv,
):
    dom, f = lax.axis_index("dom"), lax.axis_index("feat")
    core = dom % 2
    z, x = (dom // 2) % NZ, dom // (2 * NZ)
    me = 2 * x + core

    def device(zz, n):
        return {"dom": ((n // 2) * NZ + zz) * 2 + n % 2}

    rank = jnp.where(f <= NY // 2, jnp.maximum(2 * f - 1, 0), 2 * (NY - f))

    def at_rank(r):
        return {"feat": jnp.where(r % 2 == 1, (r + 1) // 2, lax.rem(NY - r // 2, NY))}

    barrier = pltpu.get_barrier_semaphore()

    def greet(device_id):
        pl.semaphore_signal(barrier, inc=1, device_id=device_id, device_id_type=MESH)

    loads = []
    for n, (src, dst) in enumerate((
        (sr_hbm, sr_v), (hr_hbm, hr_v), (x_hbm, xg.at[f]), (w_hbm, w_v), (b_hbm, b_v),
        (ls_hbm, ls_v), (ld_hbm, ld_v),
        (hs_hbm, es_v.at[pl.ds(0, 8)]), (bs_hbm, es_v.at[pl.ds(8, 8)]),
        (hd_hbm, ed_v.at[pl.ds(0, 8)]), (bd_hbm, ed_v.at[pl.ds(8, 8)]),
    )):
        copy = pltpu.make_async_copy(src, dst, in_sem.at[n])
        copy.start()
        loads.append(copy)

    for n in range(1, NG):
        greet(device(z, lax.rem(me + n, NG)))

    @pl.loop(rank + 1, NY)
    def _(r):
        greet(at_rank(r))

    @pl.loop(z + 1, NZ)
    def _(zz):
        for n in range(NG):
            greet(device(zz, n))

    row = lax.broadcasted_iota(jnp.int32, (NZ * NX * 8, 256), 0)
    col = lax.broadcasted_iota(jnp.int32, (NZ * NX * 8, 256), 1)
    t, to = row % 8, row // 8
    to = (to % NX) * NZ + to // NX
    want = jnp.where(t < 4, (t % 2) * 128 + to * 2 + t // 2, 92 + t)
    pick[...] = jnp.where(col == want, 1.0, 0.0).astype(BF)

    for copy in loads:
        copy.wait()

    lane = lax.broadcasted_iota(jnp.int32, (16, 512), 1)
    hub = lax.broadcasted_iota(jnp.int32, (16, 512), 0)
    spread = jnp.where(
        (lane // 128 == hub % 4) & (lane % 128 == 96 + hub // 4), 1.0, 0.0
    ).astype(BF)
    hub_lanes = nn(one_hot(hr_v[...], NODES), spread)
    for c in range(8):
        part = one_hot(sr_v[c : c + 1, :], NODES)
        part = jnp.concatenate([part, jnp.zeros((NODES, 32), BF)], axis=1)
        j, si = c % 4, c // 4
        if si == 0:
            part = part + hub_lanes[:, j * 128 : j * 128 + 128].astype(BF)
        ot[:, j * 256 + si * 128 : j * 256 + si * 128 + 128] = part
    own = xg[f]
    lists = jnp.concatenate(
        [nn(own, ot[:, j * 256 : j * 256 + 256]) for j in range(4)], axis=0
    ).astype(BF)
    sendb[...] = nt(pick[...], lists).reshape(NZ * NX, 8, 128).astype(BF)

    def send(zz, n, index):
        pltpu.make_async_remote_copy(
            src_ref=sendb.at[zz * NX + n // 2], dst_ref=recv.at[z, me],
            send_sem=d_send.at[index], recv_sem=d_recv.at[index if index is NZ else z],
            device_id=device(zz, n), device_id_type=MESH,
        ).start()

    def send_plane(zz):
        for n in range(NG):
            send(zz, n, zz)

    def plane_of(sem, count):
        region = recv.at[0, pl.ds(0, count)]
        return pltpu.make_async_copy(region, region, sem)

    pl.semaphore_wait(barrier, NG * z + NG - 1 + rank)

    @pl.loop(0, z)
    def _(zz):
        send_plane(zz)

    for n in range(1, NG):
        send(z, lax.rem(me + n, NG), NZ)

    @pl.loop(0, rank)
    def _(r):
        pl.semaphore_signal(ready, inc=1, device_id=at_rank(r), device_id_type=MESH)

    recv[z, me] = sendb[z * NX + x]

    def hot_rows(ref, at, out, size):
        @pl.loop(0, EDGES // 128)
        def _(i):
            lanes = pl.ds(pl.multiple_of(i * 128, 128), 128)
            out[0:size, lanes] = one_hot(ref[pl.ds(i, 1), :] - at, size)

    ls1[NODES : NODES + 16, :] = jnp.ones((16, EDGES), BF)
    es1[PART : PART + 16, :] = jnp.ones((16, EDGES), BF)
    hot_rows(ls_v, 0, ls1, NODES)
    hot_rows(ld_v, 0, ld1, NODES)
    counts = nt(ls1[...], ld1[...])
    al[...] = counts[:NODES].astype(BF)
    degree = counts[NODES : NODES + 1]
    pooled = nn(own, al[...])

    def to_peers(block, send_sem, recv_sem):
        for i in Y_ORDER:
            pltpu.make_async_remote_copy(
                src_ref=block.at[f], dst_ref=block.at[f], send_sem=send_sem, recv_sem=recv_sem,
                device_id={"feat": lax.rem(f + i, NY)}, device_id_type=MESH,
            ).start()

    def peers_of(block, sem):
        region = block.at[pl.ds(0, NY - 1)]
        return pltpu.make_async_copy(region, region, sem)

    @pl.when(rank < NY - 1)
    def _():
        pl.semaphore_wait(ready, NY - 1 - rank)

    to_peers(xg, x_send, x_recv)

    def slots(s, j, t):
        half = s // 2
        xx = half // NZ
        zz = half - xx * NZ
        line = zz * (NG * 8) + (2 * xx + s % 2) * 8 + t
        return (line // PART) * (4 * PART) + j * PART + line % PART

    h = es_v[0:8, :]
    es_v[0:8, :] = slots(h // 16, h % 4, 4 + (h // 4) % 4)
    b = es_v[8:16, :]
    es_v[8:16, :] = slots(b // 8, b % 4, 2 * core + (b // 4) % 2)

    def count_block(k):
        hot_rows(es_v, k * PART, es1, PART)
        got = nt(es1[...], ed1[...])
        ar[pl.ds(pl.multiple_of(k * PART, 16), PART), :] = got[:PART].astype(BF)
        return got[PART : PART + 1]

    hot_rows(ed_v, 0, ed1, NODES)
    degree = degree + count_block(0)

    @pl.loop(1, 4 * PARTS)
    def _(k):
        count_block(k)

    scale = 1.0 / jnp.maximum(degree, 1.0)
    diag = lax.broadcasted_iota(jnp.int32, (W, W), 0) == lax.broadcasted_iota(jnp.int32, (W, W), 1)
    bias = jnp.sum(jnp.where(diag, b_v[...].astype(F32), 0.0), axis=1, keepdims=True)
    peers_of(xg, x_recv).wait()
    own_term = nn(w_v[:, 0:256], xg[...].reshape(NY * W, NODES)) + bias
    eye = jnp.where(
        lax.broadcasted_iota(jnp.int32, (128, 128), 0)
        == lax.broadcasted_iota(jnp.int32, (128, 128), 1), 1.0, 0.0,
    ).astype(BF)

    for part in range(PARTS):
        @pl.loop(part * SPAN, part * SPAN + SPAN)
        def _(zz):
            @pl.when(zz == z)
            def _():
                plane_of(d_recv.at[NZ], NG - 1).wait()

            @pl.when(zz != z)
            def _():
                plane_of(d_recv.at[zz], NG).wait()

            @pl.when((zz > z) & (zz < NZ - 1))
            def _():
                send_plane(zz)

        rows = recv[part * SPAN : part * SPAN + SPAN].reshape(PART, 128)
        turned = nt(eye, rows).astype(BF)
        wide = jnp.concatenate([turned[j * W : j * W + W] for j in range(4)], axis=1)
        pooled = pooled + nn(wide, ar[part * 4 * PART : (part + 1) * 4 * PART, :])

    ng[f] = (pooled * scale).astype(BF)
    to_peers(ng, n_send, n_recv)

    @pl.when(z < NZ - 1)
    def _():
        send_plane(NZ - 1)

    peers_of(ng, n_recv).wait()
    out = own_term + nn(w_v[:, 256:512], ng[...].reshape(NY * W, NODES))
    o_ref[...] = jnp.maximum(out, 0.0).astype(BF)

    peers_of(xg, x_send).wait()
    peers_of(ng, n_send).wait()
    plane_of(d_send.at[NZ], NG - 1).wait()

    @pl.loop(0, NZ)
    def _(zz):
        @pl.when(zz != z)
        def _():
            plane_of(d_send.at[zz], NG).wait()


def shards(
    features, weight, bias, local_src, local_dst, hub_rows, hub_src, hub_dst, send_rows,
    bnd_src, bnd_dst,
):
    V = pltpu.VMEM
    I32 = jnp.int32
    DMA = pltpu.SemaphoreType.DMA
    out = pl.pallas_call(
        kernel,
        out_shape=jax.ShapeDtypeStruct((W, NODES), BF),
        in_specs=[pl.BlockSpec(memory_space=pl.ANY)] * 11,
        out_specs=pl.BlockSpec(memory_space=pltpu.VMEM),
        scratch_shapes=[
            V((W, NODES), BF), V((1, W), BF), V((16, 128), I32), V((16, 128), I32),
            V((1, 16), I32), V((16, 128), I32), V((16, 128), I32), V((8, 96), I32),
            V((NY, W, NODES), BF), V((NY, W, NODES), BF), V((NODES, 1024), BF),
            V((NODES, EDGES), BF), V((NODES + 16, EDGES), BF),
            V((NODES, EDGES), BF), V((PART + 16, EDGES), BF),
            V((NODES, NODES), BF), V((4 * PART * PARTS, NODES), BF), V((NZ * NX * 8, 256), BF),
            V((NZ * NX, 8, 128), BF), V((NZ, NG, 8, 128), BF),
            DMA((11,)), pltpu.SemaphoreType.REGULAR, DMA(()), DMA(()), DMA(()), DMA(()),
            DMA((NZ + 1,)), DMA((NZ + 1,)),
        ],
        compiler_params=pltpu.CompilerParams(
            collective_id=0, has_side_effects=True, vmem_limit_bytes=56 * 1024 * 1024
        ),
    )(
        features.T, weight.T, bias.reshape(1, W),
        local_src.reshape(16, 128), local_dst.reshape(16, 128), hub_rows.reshape(1, 16),
        hub_src.reshape(8, 128), hub_dst.reshape(8, 128), send_rows.T,
        bnd_src.reshape(8, 128), bnd_dst.reshape(8, 128),
    )
    return out.T


def solution(mesh):
    return jax.shard_map(
        shards,
        mesh=mesh,
        in_specs=(
            P("dom", "feat"), P(None, "feat"), P("feat"), P("dom"), P("dom"), P("dom"),
            P("dom"), P("dom"), P("dom", None), P("dom"), P("dom"),
        ),
        out_specs=P("dom", "feat"),
        check_vma=False,
    )
```

```python
import jax
import jax.numpy as jnp
from jax import lax
from jax.experimental import pallas as pl
from jax.experimental.pallas import tpu as pltpu
from jax.sharding import PartitionSpec as P

MESH = pl.DeviceIdType.MESH
BF = jnp.bfloat16
F32 = jnp.float32
NX, NZ, NY = 4, 12, 8
NG = NX * 2
NODES = 512
W = 32
EDGES = 2048
SPAN = 4
LINES = SPAN * NG * 8
PARTS = NZ // SPAN
HUB_PART = SPAN * NG * 4
BND_PART = SPAN * NG * 2
PART = 4 * (HUB_PART + BND_PART)
EARLY = 3
LATE = NZ // 2
Y_ORDER = (4, 3, 5, 2, 6, 1, 7)


def nt(a, b):
    return lax.dot_general(a, b, (((1,), (1,)), ((), ())), preferred_element_type=F32)


def nn(a, b):
    return jnp.dot(a, b, preferred_element_type=F32)


def one_hot(row, size):
    at = lax.broadcasted_iota(jnp.int32, (size, row.shape[1]), 0)
    return jnp.where(at == row, 1.0, 0.0).astype(BF)


def kernel(
    x_hbm, w_hbm, b_hbm, ls_hbm, ld_hbm, hr_hbm, hs_hbm, hd_hbm, sr_hbm, bs_hbm, bd_hbm,
    o_ref,
    w_v, b_v, ls_v, ld_v, hr_v, es_v, ed_v, sr_v, xg, ng, ot, ld1, ls1, ed1, es1, al, ar, pick,
    sel, acc, sendb, recv, in_sem, ready, x_send, x_recv, n_send, n_recv, d_send, d_recv,
):
    dom, f = lax.axis_index("dom"), lax.axis_index("feat")
    core = dom % 2
    z, x = (dom // 2) % NZ, dom // (2 * NZ)
    me = 2 * x + core

    def device(zz, n):
        return {"dom": ((n // 2) * NZ + zz) * 2 + n % 2}

    rank = jnp.where(f <= NY // 2, jnp.maximum(2 * f - 1, 0), 2 * (NY - f))

    def at_rank(r):
        return {"feat": jnp.where(r % 2 == 1, (r + 1) // 2, lax.rem(NY - r // 2, NY))}

    barrier = pltpu.get_barrier_semaphore()

    def greet(device_id):
        pl.semaphore_signal(barrier, inc=1, device_id=device_id, device_id_type=MESH)

    loads = []
    for n, (src, dst) in enumerate((
        (sr_hbm, sr_v), (hr_hbm, hr_v), (x_hbm, xg.at[f]), (w_hbm, w_v), (b_hbm, b_v),
        (ls_hbm, ls_v), (ld_hbm, ld_v),
        (hs_hbm, es_v.at[pl.ds(0, 8)]), (bs_hbm, es_v.at[pl.ds(8, 8)]),
        (hd_hbm, ed_v.at[pl.ds(0, 8)]), (bd_hbm, ed_v.at[pl.ds(8, 8)]),
    )):
        copy = pltpu.make_async_copy(src, dst, in_sem.at[n])
        copy.start()
        loads.append(copy)

    for n in range(1, NG):
        greet(device(z, lax.rem(me + n, NG)))

    @pl.loop(rank + 1, NY)
    def _(r):
        greet(at_rank(r))

    def greet_up():
        @pl.loop(z + 1, NZ)
        def _(zz):
            for n in range(NG):
                greet(device(zz, n))

    pl.when(z >= EARLY)(greet_up)

    row = lax.broadcasted_iota(jnp.int32, (NZ * NX * 8, 256), 0)
    col = lax.broadcasted_iota(jnp.int32, (NZ * NX * 8, 256), 1)
    t, to = row % 8, row // 8
    to = (to % NX) * NZ + to // NX
    want = jnp.where(t < 4, (t % 2) * 128 + to * 2 + t // 2, 92 + t)
    pick[...] = jnp.where(col == want, 1.0, 0.0).astype(BF)

    for copy in loads:
        copy.wait()

    lane = lax.broadcasted_iota(jnp.int32, (16, 512), 1)
    hub = lax.broadcasted_iota(jnp.int32, (16, 512), 0)
    spread = jnp.where(
        (lane // 128 == hub % 4) & (lane % 128 == 96 + hub // 4), 1.0, 0.0
    ).astype(BF)
    hub_lanes = nn(one_hot(hr_v[...], NODES), spread)
    for c in range(8):
        part = one_hot(sr_v[c : c + 1, :], NODES)
        part = jnp.concatenate([part, jnp.zeros((NODES, 32), BF)], axis=1)
        j, si = c % 4, c // 4
        if si == 0:
            part = part + hub_lanes[:, j * 128 : j * 128 + 128].astype(BF)
        ot[:, j * 256 + si * 128 : j * 256 + si * 128 + 128] = part
    own = xg[f]
    lists = jnp.concatenate(
        [nn(own, ot[:, j * 256 : j * 256 + 256]) for j in range(4)], axis=0
    ).astype(BF)
    sendb[...] = nt(pick[...], lists).reshape(NZ * NX, 8, 128).astype(BF)

    def send(zz, n, index):
        pltpu.make_async_remote_copy(
            src_ref=sendb.at[zz * NX + n // 2], dst_ref=recv.at[z, me],
            send_sem=d_send.at[index], recv_sem=d_recv.at[index if index is NZ else z],
            device_id=device(zz, n), device_id_type=MESH,
        ).start()

    def send_plane(zz):
        for n in range(NG):
            send(zz, n, zz)

    def plane_of(sem, count):
        region = recv.at[0, pl.ds(0, count)]
        return pltpu.make_async_copy(region, region, sem)

    pl.semaphore_wait(barrier, NG * z + NG - 1 + rank)

    @pl.loop(0, z)
    def _(zz):
        send_plane(zz)

    for n in range(1, NG):
        send(z, lax.rem(me + n, NG), NZ)

    @pl.loop(0, rank)
    def _(r):
        pl.semaphore_signal(ready, inc=1, device_id=at_rank(r), device_id_type=MESH)

    pl.when(z < EARLY)(greet_up)

    recv[z, me] = sendb[z * NX + x]

    def hot_rows(ref, at, out, size, first=0):
        @pl.loop(0, out.shape[1] // 128)
        def _(i):
            lanes = pl.ds(pl.multiple_of(i * 128, 128), 128)
            out[0:size, lanes] = one_hot(ref[pl.ds(first + i, 1), :] - at, size)

    ls1[NODES : NODES + 16, :] = jnp.ones((16, EDGES), BF)
    es1[4 * HUB_PART : 4 * HUB_PART + 16, :] = jnp.ones((16, EDGES // 2), BF)
    hot_rows(ls_v, 0, ls1, NODES)
    hot_rows(ld_v, 0, ld1, NODES)
    counts = nt(ls1[...], ld1[...])
    al[...] = counts[:NODES].astype(BF)
    degree = counts[NODES : NODES + 1]
    pooled = nn(own, al[...])

    def to_peers(block, send_sem, recv_sem):
        for i in Y_ORDER:
            pltpu.make_async_remote_copy(
                src_ref=block.at[f], dst_ref=block.at[f], send_sem=send_sem, recv_sem=recv_sem,
                device_id={"feat": lax.rem(f + i, NY)}, device_id_type=MESH,
            ).start()

    def peers_of(block, sem):
        region = block.at[pl.ds(0, NY - 1)]
        return pltpu.make_async_copy(region, region, sem)

    @pl.when(rank < NY - 1)
    def _():
        pl.semaphore_wait(ready, NY - 1 - rank)

    to_peers(xg, x_send, x_recv)

    def slots(s, j, position, width):
        half = s // 2
        xx = half // NZ
        zz = half - xx * NZ
        size = SPAN * NG * width
        line = (zz * NG + 2 * xx + s % 2) * width + position
        return (line // size) * (4 * size) + j * size + line % size

    h = es_v[0:8, :]
    es_v[0:8, :] = slots(h // 16, h % 4, (h // 4) % 4, 4)
    b = es_v[8:16, :]
    es_v[8:16, :] = slots(b // 8, b % 4, (b // 4) % 2, 2)

    hot_rows(ed_v, 0, ed1, NODES)
    hot_rows(es_v, 0, es1, 4 * HUB_PART)
    got = nt(es1[...], ed1[...])
    ar[0 : 4 * HUB_PART, :] = got[: 4 * HUB_PART].astype(BF)
    degree = degree + got[4 * HUB_PART : 4 * HUB_PART + 1]

    for k in range(1, PARTS):
        hot_rows(es_v, k * (4 * HUB_PART), es1, 4 * HUB_PART)
        got = nt(es1[0 : 4 * HUB_PART, :], ed1[...])
        ar[pl.ds(k * PART, 4 * HUB_PART), :] = got.astype(BF)

    half = 4 * BND_PART
    hot_rows(ed_v, 0, ed1, NODES, 8)
    degree = degree + nt(es1[4 * HUB_PART : 4 * HUB_PART + 16, :], ed1[...])[0:1]

    for k in range(PARTS):
        hot_rows(es_v, k * half, es1, half, 8)
        got = nt(es1[0:half, :], ed1[...])
        ar[pl.ds(k * PART + 4 * HUB_PART, half), :] = got.astype(BF)

    scale = 1.0 / jnp.maximum(degree, 1.0)
    acc[...] = pooled
    diag = lax.broadcasted_iota(jnp.int32, (W, W), 0) == lax.broadcasted_iota(jnp.int32, (W, W), 1)
    bias = jnp.sum(jnp.where(diag, b_v[...].astype(F32), 0.0), axis=1, keepdims=True)
    eye = jnp.where(
        lax.broadcasted_iota(jnp.int32, (128, 128), 0)
        == lax.broadcasted_iota(jnp.int32, (128, 128), 1), 1.0, 0.0,
    ).astype(BF)
    line = lax.broadcasted_iota(jnp.int32, (LINES, 256), 0)
    at = lax.broadcasted_iota(jnp.int32, (LINES, 256), 1)
    low = at - HUB_PART
    want = jnp.where(low < 0, (at // 4) * 8 + 4 + at % 4, (low // 2) * 8 + 2 * core + low % 2)
    sel[...] = jnp.where((line == want) & (low < BND_PART), 1.0, 0.0).astype(BF)

    def pool(part):
        rows = recv[part * SPAN : part * SPAN + SPAN].reshape(LINES, 128)
        turned = nn(nt(eye, rows).astype(BF), sel[...]).astype(BF)
        wide = jnp.concatenate(
            [turned[j * W : j * W + W, 0:HUB_PART] for j in range(4)]
            + [turned[j * W : j * W + W, HUB_PART : HUB_PART + BND_PART] for j in range(4)],
            axis=1,
        )
        acc[...] += nn(wide, ar[part * PART : (part + 1) * PART, :])

    def arrive(zz):
        plane_of(d_recv.at[zz], NG).wait()

    def arrive_and_answer(zz):
        arrive(zz)
        send_plane(zz)

    @pl.when(z == 0)
    def _():
        plane_of(d_recv.at[NZ], NG - 1).wait()
        pl.loop(1, SPAN)(arrive_and_answer)

    @pl.when(z > 0)
    def _():
        @pl.when(z < LATE)
        def _():
            pl.loop(z + 1, LATE)(arrive_and_answer)
            pl.loop(LATE, NZ)(arrive)

        @pl.when(z >= LATE)
        def _():
            pl.loop(z + 1, NZ)(arrive_and_answer)

        plane_of(d_recv.at[NZ], NG - 1).wait()
        pl.loop(0, z)(arrive)

    pool(0)

    @pl.when(z == 0)
    def _():
        pl.loop(SPAN, LATE)(arrive_and_answer)
        pl.loop(LATE, 2 * SPAN)(arrive)

    pool(1)

    @pl.when(z == 0)
    def _():
        pl.loop(2 * SPAN, NZ)(arrive)

    pool(2)

    ng[f] = (acc[...] * scale).astype(BF)
    to_peers(ng, n_send, n_recv)

    @pl.when(z < LATE)
    def _():
        pl.loop(LATE, NZ)(send_plane)

    peers_of(xg, x_recv).wait()
    own_term = nn(w_v[:, 0:256], xg[...].reshape(NY * W, NODES)) + bias
    peers_of(ng, n_recv).wait()
    out = own_term + nn(w_v[:, 256:512], ng[...].reshape(NY * W, NODES))
    o_ref[...] = jnp.maximum(out, 0.0).astype(BF)

    peers_of(xg, x_send).wait()
    peers_of(ng, n_send).wait()
    plane_of(d_send.at[NZ], NG - 1).wait()

    @pl.loop(0, NZ)
    def _(zz):
        @pl.when(zz != z)
        def _():
            plane_of(d_send.at[zz], NG).wait()


def shards(
    features, weight, bias, local_src, local_dst, hub_rows, hub_src, hub_dst, send_rows,
    bnd_src, bnd_dst,
):
    V = pltpu.VMEM
    I32 = jnp.int32
    DMA = pltpu.SemaphoreType.DMA
    out = pl.pallas_call(
        kernel,
        out_shape=jax.ShapeDtypeStruct((W, NODES), BF),
        in_specs=[pl.BlockSpec(memory_space=pl.ANY)] * 11,
        out_specs=pl.BlockSpec(memory_space=pltpu.VMEM),
        scratch_shapes=[
            V((W, NODES), BF), V((1, W), BF), V((16, 128), I32), V((16, 128), I32),
            V((1, 16), I32), V((16, 128), I32), V((16, 128), I32), V((8, 96), I32),
            V((NY, W, NODES), BF), V((NY, W, NODES), BF), V((NODES, 1024), BF),
            V((NODES, EDGES), BF), V((NODES + 16, EDGES), BF),
            V((NODES, EDGES // 2), BF), V((4 * HUB_PART + 16, EDGES // 2), BF),
            V((NODES, NODES), BF), V((PART * PARTS, NODES), BF), V((NZ * NX * 8, 256), BF),
            V((LINES, 256), BF), V((W, NODES), F32),
            V((NZ * NX, 8, 128), BF), V((NZ, NG, 8, 128), BF),
            DMA((11,)), pltpu.SemaphoreType.REGULAR, DMA(()), DMA(()), DMA(()), DMA(()),
            DMA((NZ + 1,)), DMA((NZ + 1,)),
        ],
        compiler_params=pltpu.CompilerParams(
            collective_id=0, has_side_effects=True, vmem_limit_bytes=56 * 1024 * 1024
        ),
    )(
        features.T, weight.T, bias.reshape(1, W),
        local_src.reshape(16, 128), local_dst.reshape(16, 128), hub_rows.reshape(1, 16),
        hub_src.reshape(8, 128), hub_dst.reshape(8, 128), send_rows.T,
        bnd_src.reshape(8, 128), bnd_dst.reshape(8, 128),
    )
    return out.T


def solution(mesh):
    return jax.shard_map(
        shards,
        mesh=mesh,
        in_specs=(
            P("dom", "feat"), P(None, "feat"), P("feat"), P("dom"), P("dom"), P("dom"),
            P("dom"), P("dom"), P("dom", None), P("dom"), P("dom"),
        ),
        out_specs=P("dom", "feat"),
        check_vma=False,
    )
```

```python
import jax
import jax.numpy as jnp
from jax import lax
from jax.experimental import pallas as pl
from jax.experimental.pallas import tpu as pltpu
from jax.sharding import PartitionSpec as P

MESH = pl.DeviceIdType.MESH
BF = jnp.bfloat16
F32 = jnp.float32
NX, NZ, NY = 4, 12, 8
NQ = NX * NZ
NODES = 512
W = 32
EDGES = 2048
ROWS = NQ * 8
HUBS = NQ * 4
BNDS = NQ * 2
LINES = HUBS + BNDS


def nt(a, b):
    return lax.dot_general(a, b, (((1,), (1,)), ((), ())), preferred_element_type=F32)


def nn(a, b):
    return jnp.dot(a, b, preferred_element_type=F32)


def one_hot(row, size):
    at = lax.broadcasted_iota(jnp.int32, (size, row.shape[1]), 0)
    return jnp.where(at == row, 1.0, 0.0).astype(BF)


def kernel(
    x_hbm, w_hbm, b_hbm, ls_hbm, ld_hbm, hr_hbm, hs_hbm, hd_hbm, sr_hbm, bs_hbm, bd_hbm,
    o_ref,
    w_v, b_v, ls_v, ld_v, hr_v, es_v, ed_v, sr_v, xg, ot, ld1, ls1, ed1, es1, al, ar, pick, sel,
    sendb, recv, in_sem, ready, heard, all_in, y_send, y_recv, d_send, d_recv, c_send, c_recv,
):
    dom, f = lax.axis_index("dom"), lax.axis_index("feat")
    core = dom % 2
    q = dom // 2
    z, x = q % NZ, q // NZ

    def chip(xx, zz):
        return {"dom": (xx * NZ + zz) * 2 + core}

    sibling = {"dom": q * 2 + (1 - core)}

    rank = jnp.where(f <= NY // 2, jnp.maximum(2 * f - 1, 0), 2 * (NY - f))

    def at_rank(r):
        return {"feat": jnp.where(r % 2 == 1, (r + 1) // 2, lax.rem(NY - r // 2, NY))}

    def signal(sem, device_id):
        pl.semaphore_signal(sem, inc=1, device_id=device_id, device_id_type=MESH)

    loads = []
    for n, (src, dst) in enumerate((
        (x_hbm, xg.at[f]), (sr_hbm, sr_v), (hr_hbm, hr_v), (w_hbm, w_v), (b_hbm, b_v),
        (ls_hbm, ls_v), (ld_hbm, ld_v),
        (hs_hbm, es_v.at[pl.ds(0, 8)]), (bs_hbm, es_v.at[pl.ds(8, 8)]),
        (hd_hbm, ed_v.at[pl.ds(0, 8)]), (bd_hbm, ed_v.at[pl.ds(8, 8)]),
    )):
        copy = pltpu.make_async_copy(src, dst, in_sem.at[n])
        copy.start()
        loads.append(copy)

    barrier = pltpu.get_barrier_semaphore()
    signal(barrier, sibling)

    @pl.loop(rank + 1, NY)
    def _(r):
        signal(barrier, at_rank(r))

    @pl.when(z == 0)
    def _():
        for dx in range(1, NX):
            signal(barrier, chip(lax.rem(x + dx, NX), 0))

        @pl.loop(1, NZ)
        def _(zz):
            for xx in range(NX):
                signal(barrier, chip(xx, zz))

    pl.semaphore_wait(barrier, 1 + rank + jnp.where(z == 0, NX - 1, NX))

    @pl.when(z > 0)
    def _():
        for xx in range(NX):
            signal(heard, chip(xx, 0))

    @pl.loop(0, rank)
    def _(r):
        signal(ready.at[rank], at_rank(r))

    def send_x(r):
        pltpu.make_async_remote_copy(
            src_ref=xg.at[f], dst_ref=xg.at[f], send_sem=y_send, recv_sem=y_recv,
            device_id=at_rank(r), device_id_type=MESH,
        ).start()

    loads[0].wait()
    pl.loop(0, rank)(send_x)
    for copy in loads[1:]:
        copy.wait()

    lane = lax.broadcasted_iota(jnp.int32, (16, 512), 1)
    hub = lax.broadcasted_iota(jnp.int32, (16, 512), 0)
    spread = jnp.where(
        (lane // 128 == hub % 4) & (lane % 128 == 96 + hub // 4), 1.0, 0.0
    ).astype(BF)
    hub_lanes = nn(one_hot(hr_v[...], NODES), spread)
    for c in range(8):
        part = one_hot(sr_v[c : c + 1, :], NODES)
        part = jnp.concatenate([part, jnp.zeros((NODES, 32), BF)], axis=1)
        j, si = c % 4, c // 4
        if si == 0:
            part = part + hub_lanes[:, j * 128 : j * 128 + 128].astype(BF)
        ot[:, j * 256 + si * 128 : j * 256 + si * 128 + 128] = part
    row = lax.broadcasted_iota(jnp.int32, (ROWS, 256), 0)
    col = lax.broadcasted_iota(jnp.int32, (ROWS, 256), 1)
    t = row % 8
    want = jnp.where(t < 4, (t % 2) * 128 + (row // 8) * 2 + t // 2, 92 + t)
    pick[...] = jnp.where(col == want, 1.0, 0.0).astype(BF)
    line = lax.broadcasted_iota(jnp.int32, (ROWS, LINES), 0)
    at = lax.broadcasted_iota(jnp.int32, (ROWS, LINES), 1)
    low = at - HUBS
    want = jnp.where(low < 0, (at // 4) * 8 + 4 + at % 4, (low // 2) * 8 + 2 * core + low % 2)
    sel[...] = jnp.where(line == want, 1.0, 0.0).astype(BF)

    def hot_rows(ref, at, out, size, first=0):
        @pl.loop(0, out.shape[1] // 128)
        def _(i):
            lanes = pl.ds(pl.multiple_of(i * 128, 128), 128)
            out[0:size, lanes] = one_hot(ref[pl.ds(first + i, 1), :] - at, size)

    ls1[NODES : NODES + 16, :] = jnp.ones((16, EDGES), BF)
    es1[4 * HUBS : 4 * HUBS + 16, :] = jnp.ones((16, EDGES // 2), BF)
    hot_rows(ls_v, 0, ls1, NODES)
    hot_rows(ld_v, 0, ld1, NODES)
    counts = nt(ls1[...], ld1[...])
    al[...] = counts[:NODES].astype(BF)
    degree = counts[NODES : NODES + 1]

    @pl.loop(rank + 1, NY)
    def _(r):
        pl.semaphore_wait(ready.at[r], 1)
        send_x(r)

    h = es_v[0:8, :]
    s = h // 16
    es_v[0:8, :] = (s % 2) * (4 * HUBS) + (h % 4) * HUBS + (s // 2) * 4 + (h // 4) % 4
    b = es_v[8:16, :]
    s = b // 8
    es_v[8:16, :] = (s % 2) * (4 * BNDS) + (b % 4) * BNDS + (s // 2) * 2 + (b // 4) % 2

    hot_rows(ed_v, 0, ed1, NODES)
    for side in range(2):
        hot_rows(es_v, side * (4 * HUBS), es1, 4 * HUBS)
        got = nt(es1[...], ed1[...])
        for j in range(4):
            base = (side * 4 + j) * LINES
            ar[base : base + HUBS, :] = got[j * HUBS : (j + 1) * HUBS].astype(BF)
    degree = degree + got[4 * HUBS : 4 * HUBS + 1]
    hot_rows(ed_v, 0, ed1, NODES, 8)
    for side in range(2):
        hot_rows(es_v, side * (4 * BNDS), es1, 4 * BNDS, 8)
        got = nt(es1[0 : 4 * BNDS, :], ed1[...])
        for j in range(4):
            base = (side * 4 + j) * LINES + HUBS
            ar[base : base + BNDS, :] = got[j * BNDS : (j + 1) * BNDS].astype(BF)
    degree = degree + nt(es1[4 * HUBS : 4 * HUBS + 16, :], ed1[...])[0:1]
    scale = 1.0 / jnp.maximum(degree, 1.0)
    diag = lax.broadcasted_iota(jnp.int32, (W, W), 0) == lax.broadcasted_iota(jnp.int32, (W, W), 1)
    bias = jnp.sum(jnp.where(diag, b_v[...].astype(F32), 0.0), axis=1, keepdims=True)
    eye = jnp.where(
        lax.broadcasted_iota(jnp.int32, (128, 128), 0)
        == lax.broadcasted_iota(jnp.int32, (128, 128), 1), 1.0, 0.0,
    ).astype(BF)

    def all_of(region, sem):
        return pltpu.make_async_copy(region, region, sem)

    others = xg.at[pl.ds(0, NY - 1)]
    all_of(others, y_recv).wait()

    both = jnp.concatenate([w_v[:, 256:512], w_v[:, 0:256]], axis=0)
    yz = nn(both, xg[...].reshape(NY * W, NODES))
    high = yz[0:W].astype(BF)
    lists = jnp.concatenate(
        [nn(high, ot[:, j * 256 : j * 256 + 256]) for j in range(4)], axis=0
    ).astype(BF)
    sendb[...] = nt(pick[...], lists).reshape(NQ, 8, 128).astype(BF)
    recv[core, q] = sendb[q]

    @pl.when(z == 0)
    def _():
        pl.semaphore_wait(heard, NX * (NZ - 1))

        @pl.when(x > 0)
        def _():
            @pl.loop(0, NZ - 1)
            def _(i):
                zz = lax.rem(i + 5, NZ - 1) + 1
                signal(all_in, chip(x, zz))

                @pl.when(x == 1)
                def _():
                    signal(all_in, chip(0, zz))

    @pl.when(z > 0)
    def _():
        pl.semaphore_wait(all_in, 1)

    def send_rows_to(xx, zz):
        pltpu.make_async_remote_copy(
            src_ref=sendb.at[xx * NZ + zz], dst_ref=recv.at[core, q], send_sem=d_send,
            recv_sem=d_recv, device_id=chip(xx, zz), device_id_type=MESH,
        ).start()

    @pl.loop(0, NZ)
    def _(zz):
        for dx in range(1, NX):
            send_rows_to(lax.rem(x + dx, NX), zz)

        @pl.when(zz != z)
        def _():
            send_rows_to(x, zz)

    low_y = (yz[0:W] - high.astype(F32)).astype(BF)
    near = nn(jnp.concatenate([high, low_y], axis=0), al[...])
    pooled = near[0:W] + near[W : 2 * W]

    def add_half(side):
        rows = recv[side].reshape(ROWS, 128)
        turned = nn(nt(eye, rows).astype(BF), sel[...]).astype(BF)
        wide = jnp.concatenate([turned[j * W : j * W + W] for j in range(4)], axis=1)
        return nn(wide, ar[pl.ds(pl.multiple_of(side * (4 * LINES), 16), 4 * LINES), :])

    rest = recv.at[0, pl.ds(0, NQ - 1)]
    all_of(rest, d_recv).wait()
    swap = pltpu.make_async_remote_copy(
        src_ref=recv.at[core], dst_ref=recv.at[core], send_sem=c_send, recv_sem=c_recv,
        device_id=sibling, device_id_type=MESH,
    )
    swap.start()
    pooled = pooled + add_half(core)
    swap.wait_recv()
    pooled = pooled + add_half(1 - core)

    out = yz[W : 2 * W] + bias + pooled * scale
    o_ref[...] = jnp.maximum(out, 0.0).astype(BF)
    all_of(others, y_send).wait()
    all_of(rest, d_send).wait()
    swap.wait_send()


def shards(
    features, weight, bias, local_src, local_dst, hub_rows, hub_src, hub_dst, send_rows,
    bnd_src, bnd_dst,
):
    V = pltpu.VMEM
    I32 = jnp.int32
    DMA = pltpu.SemaphoreType.DMA
    REGULAR = pltpu.SemaphoreType.REGULAR
    out = pl.pallas_call(
        kernel,
        out_shape=jax.ShapeDtypeStruct((W, NODES), BF),
        in_specs=[pl.BlockSpec(memory_space=pl.ANY)] * 11,
        out_specs=pl.BlockSpec(memory_space=pltpu.VMEM),
        scratch_shapes=[
            V((W, NODES), BF), V((1, W), BF), V((16, 128), I32), V((16, 128), I32),
            V((1, 16), I32), V((16, 128), I32), V((16, 128), I32), V((8, 96), I32),
            V((NY, W, NODES), BF), V((NODES, 1024), BF),
            V((NODES, EDGES), BF), V((NODES + 16, EDGES), BF),
            V((NODES, EDGES // 2), BF), V((4 * HUBS + 16, EDGES // 2), BF),
            V((NODES, NODES), BF), V((8 * LINES, NODES), BF), V((ROWS, 256), BF),
            V((ROWS, LINES), BF), V((NQ, 8, 128), BF), V((2, NQ, 8, 128), BF),
            DMA((11,)), REGULAR((NY,)), REGULAR, REGULAR, DMA(()), DMA(()), DMA(()), DMA(()),
            DMA(()), DMA(()),
        ],
        compiler_params=pltpu.CompilerParams(
            collective_id=0, has_side_effects=True, vmem_limit_bytes=56 * 1024 * 1024
        ),
    )(
        features.T, weight.T, bias.reshape(1, W),
        local_src.reshape(16, 128), local_dst.reshape(16, 128), hub_rows.reshape(1, 16),
        hub_src.reshape(8, 128), hub_dst.reshape(8, 128), send_rows.T,
        bnd_src.reshape(8, 128), bnd_dst.reshape(8, 128),
    )
    return out.T


def solution(mesh):
    return jax.shard_map(
        shards,
        mesh=mesh,
        in_specs=(
            P("dom", "feat"), P(None, "feat"), P("feat"), P("dom"), P("dom"), P("dom"),
            P("dom"), P("dom"), P("dom", None), P("dom"), P("dom"),
        ),
        out_specs=P("dom", "feat"),
        check_vma=False,
    )
```

```python
import jax
import jax.numpy as jnp
from jax import lax
from jax.experimental import pallas as pl
from jax.experimental.pallas import tpu as pltpu
from jax.sharding import PartitionSpec as P

MESH = pl.DeviceIdType.MESH
BF = jnp.bfloat16
F32 = jnp.float32
NX, NZ, NY = 4, 12, 8
NQ = NX * NZ
NODES = 512
W = 32
EDGES = 2048
ROWS = NQ * 8
HUBS = NQ * 4
BNDS = NQ * 2
LINES = HUBS + BNDS
DIRECT = 3
Y_ORDER = (4, 3, 5, 2, 6, 1, 7)


def nt(a, b):
    return lax.dot_general(a, b, (((1,), (1,)), ((), ())), preferred_element_type=F32)


def nn(a, b):
    return jnp.dot(a, b, preferred_element_type=F32)


def one_hot(row, size):
    at = lax.broadcasted_iota(jnp.int32, (size, row.shape[1]), 0)
    return jnp.where(at == row, 1.0, 0.0).astype(BF)


def kernel(
    x_hbm, w_hbm, b_hbm, ls_hbm, ld_hbm, hr_hbm, hs_hbm, hd_hbm, sr_hbm, bs_hbm, bd_hbm,
    o_ref,
    w_v, b_v, ls_v, ld_v, hr_v, es_v, ed_v, sr_v, xg, ot, ld1, ls1, ed1, es1, al, ar, pick, sel,
    sendb, recv, in_sem, heard, all_in, y_send, y_recv, d_send, d_recv, c_send, c_recv,
):
    dom, f = lax.axis_index("dom"), lax.axis_index("feat")
    core = dom % 2
    q = dom // 2
    z, x = q % NZ, q // NZ

    def chip(xx, zz, on=core):
        return {"dom": (xx * NZ + zz) * 2 + on}

    other = 1 - core
    sibling = chip(x, z, other)

    def peer(i):
        return {"feat": lax.rem(f + i, NY)}

    def signal(sem, device_id):
        pl.semaphore_signal(sem, inc=1, device_id=device_id, device_id_type=MESH)

    loads = []
    for n, (src, dst) in enumerate((
        (x_hbm, xg.at[f]), (sr_hbm, sr_v), (hr_hbm, hr_v), (w_hbm, w_v), (b_hbm, b_v),
        (ls_hbm, ls_v), (ld_hbm, ld_v),
        (hs_hbm, es_v.at[pl.ds(0, 8)]), (bs_hbm, es_v.at[pl.ds(8, 8)]),
        (hd_hbm, ed_v.at[pl.ds(0, 8)]), (bd_hbm, ed_v.at[pl.ds(8, 8)]),
    )):
        copy = pltpu.make_async_copy(src, dst, in_sem.at[n])
        copy.start()
        loads.append(copy)

    barrier = pltpu.get_barrier_semaphore()
    for i in Y_ORDER:
        signal(barrier, peer(i))
    signal(barrier, sibling)

    @pl.when(z == 0)
    def _():
        for dx in range(1, NX):
            for on in range(2):
                signal(barrier, chip(lax.rem(x + dx, NX), 0, on))

        @pl.loop(0, NZ - 1)
        def _(i):
            for xx in range(NX):
                for on in range(2):
                    signal(barrier, chip(xx, lax.rem(i + 5, NZ - 1) + 1, on))

    pl.semaphore_wait(barrier, NY + jnp.where(z == 0, 2 * NX - 2, 2 * NX))

    loads[0].wait()
    for i in Y_ORDER:
        pltpu.make_async_remote_copy(
            src_ref=xg.at[f], dst_ref=xg.at[f], send_sem=y_send, recv_sem=y_recv,
            device_id=peer(i), device_id_type=MESH,
        ).start()

    @pl.when(z > 0)
    def _():
        for xx in range(NX):
            signal(heard, chip(xx, 0))

    for copy in loads[1:]:
        copy.wait()

    lane = lax.broadcasted_iota(jnp.int32, (16, 512), 1)
    hub = lax.broadcasted_iota(jnp.int32, (16, 512), 0)
    spread = jnp.where(
        (lane // 128 == hub % 4) & (lane % 128 == 96 + hub // 4), 1.0, 0.0
    ).astype(BF)
    hub_lanes = nn(one_hot(hr_v[...], NODES), spread)
    for c in range(8):
        part = one_hot(sr_v[c : c + 1, :], NODES)
        part = jnp.concatenate([part, jnp.zeros((NODES, 32), BF)], axis=1)
        j, si = c % 4, c // 4
        if si == 0:
            part = part + hub_lanes[:, j * 128 : j * 128 + 128].astype(BF)
        ot[:, j * 256 + si * 128 : j * 256 + si * 128 + 128] = part
    row = lax.broadcasted_iota(jnp.int32, (ROWS, 256), 0)
    col = lax.broadcasted_iota(jnp.int32, (ROWS, 256), 1)
    t = row % 8
    want = jnp.where(t < 4, (t % 2) * 128 + (row // 8) * 2 + t // 2, 92 + t)
    pick[...] = jnp.where(col == want, 1.0, 0.0).astype(BF)
    line = lax.broadcasted_iota(jnp.int32, (ROWS, LINES), 0)
    at = lax.broadcasted_iota(jnp.int32, (ROWS, LINES), 1)
    low = at - HUBS
    want = jnp.where(low < 0, (at // 4) * 8 + 4 + at % 4, (low // 2) * 8 + 2 * core + low % 2)
    sel[...] = jnp.where(line == want, 1.0, 0.0).astype(BF)

    def hot_rows(ref, at, out, size, first=0):
        @pl.loop(0, out.shape[1] // 128)
        def _(i):
            lanes = pl.ds(pl.multiple_of(i * 128, 128), 128)
            out[0:size, lanes] = one_hot(ref[pl.ds(first + i, 1), :] - at, size)

    ls1[NODES : NODES + 16, :] = jnp.ones((16, EDGES), BF)
    es1[4 * HUBS : 4 * HUBS + 16, :] = jnp.ones((16, EDGES // 2), BF)
    hot_rows(ls_v, 0, ls1, NODES)
    hot_rows(ld_v, 0, ld1, NODES)
    counts = nt(ls1[...], ld1[...])
    al[...] = counts[:NODES].astype(BF)
    degree = counts[NODES : NODES + 1]

    h = es_v[0:8, :]
    s = h // 16
    es_v[0:8, :] = (s % 2) * (4 * HUBS) + (h % 4) * HUBS + (s // 2) * 4 + (h // 4) % 4
    b = es_v[8:16, :]
    s = b // 8
    es_v[8:16, :] = (s % 2) * (4 * BNDS) + (b % 4) * BNDS + (s // 2) * 2 + (b // 4) % 2

    hot_rows(ed_v, 0, ed1, NODES)
    for side in range(2):
        hot_rows(es_v, side * (4 * HUBS), es1, 4 * HUBS)
        got = nt(es1[...], ed1[...])
        for j in range(4):
            base = (side * 4 + j) * LINES
            ar[base : base + HUBS, :] = got[j * HUBS : (j + 1) * HUBS].astype(BF)
    degree = degree + got[4 * HUBS : 4 * HUBS + 1]
    diag = lax.broadcasted_iota(jnp.int32, (W, W), 0) == lax.broadcasted_iota(jnp.int32, (W, W), 1)
    bias = jnp.sum(jnp.where(diag, b_v[...].astype(F32), 0.0), axis=1, keepdims=True)
    eye = jnp.where(
        lax.broadcasted_iota(jnp.int32, (128, 128), 0)
        == lax.broadcasted_iota(jnp.int32, (128, 128), 1), 1.0, 0.0,
    ).astype(BF)

    def all_of(region, sem):
        return pltpu.make_async_copy(region, region, sem)

    others = xg.at[pl.ds(0, NY - 1)]
    all_of(others, y_recv).wait()

    both = jnp.concatenate([w_v[:, 256:512], w_v[:, 0:256]], axis=0)
    yz = nn(both, xg[...].reshape(NY * W, NODES))
    high = yz[0:W].astype(BF)
    lists = jnp.concatenate(
        [nn(high, ot[:, j * 256 : j * 256 + 256]) for j in range(4)], axis=0
    ).astype(BF)
    sendb[...] = nt(pick[...], lists).reshape(NQ, 8, 128).astype(BF)
    recv[core, q] = sendb[q]

    @pl.when(z == 0)
    def _():
        pl.semaphore_wait(heard, NX * (NZ - 1))

        @pl.when(x > 0)
        def _():
            @pl.loop(0, NZ - 1)
            def _(i):
                zz = lax.rem(i + 5, NZ - 1) + 1
                signal(all_in, chip(x, zz))

                @pl.when(x == 1)
                def _():
                    signal(all_in, chip(0, zz))

    def send_rows_to(xx, zz, on=core):
        pltpu.make_async_remote_copy(
            src_ref=sendb.at[xx * NZ + zz], dst_ref=recv.at[core, q], send_sem=d_send.at[0],
            recv_sem=d_recv.at[0], device_id=chip(xx, zz, on), device_id_type=MESH,
        ).start()

    def send_across(xx, zz):
        pltpu.make_async_remote_copy(
            src_ref=sendb.at[xx * NZ + zz], dst_ref=recv.at[core, q], send_sem=d_send.at[1],
            recv_sem=d_recv.at[1], device_id=chip(xx, zz, other), device_id_type=MESH,
        ).start()

    def send_plane(zz):
        for dx in range(1, NX):
            send_rows_to(lax.rem(x + dx, NX), zz)

        @pl.when(zz != z)
        def _():
            send_rows_to(x, zz)

    def send_first_plane(zz):
        send_plane(zz)
        for xx in range(NX):
            send_across(xx, zz)

    send_first_plane(0)

    @pl.when(z > 0)
    def _():
        pl.semaphore_wait(all_in, 1)

    pl.loop(1, DIRECT)(send_first_plane)
    pl.loop(DIRECT, NZ)(send_plane)

    hot_rows(ed_v, 0, ed1, NODES, 8)
    for side in range(2):
        hot_rows(es_v, side * (4 * BNDS), es1, 4 * BNDS, 8)
        got = nt(es1[0 : 4 * BNDS, :], ed1[...])
        for j in range(4):
            base = (side * 4 + j) * LINES + HUBS
            ar[base : base + BNDS, :] = got[j * BNDS : (j + 1) * BNDS].astype(BF)
    degree = degree + nt(es1[4 * HUBS : 4 * HUBS + 16, :], ed1[...])[0:1]
    scale = 1.0 / jnp.maximum(degree, 1.0)
    low_y = (yz[0:W] - high.astype(F32)).astype(BF)
    near = nn(jnp.concatenate([high, low_y], axis=0), al[...])
    pooled = near[0:W] + near[W : 2 * W]

    def add_half(side):
        rows = recv[side].reshape(ROWS, 128)
        turned = nn(nt(eye, rows).astype(BF), sel[...]).astype(BF)
        wide = jnp.concatenate([turned[j * W : j * W + W] for j in range(4)], axis=1)
        return nn(wide, ar[pl.ds(pl.multiple_of(side * (4 * LINES), 16), 4 * LINES), :])

    rest = recv.at[0, pl.ds(0, NQ - 1)]
    all_of(rest, d_recv.at[0]).wait()
    swap = pltpu.make_async_remote_copy(
        src_ref=recv.at[core], dst_ref=recv.at[core], send_sem=c_send, recv_sem=c_recv,
        device_id=sibling, device_id_type=MESH,
    )
    pl.when(z >= DIRECT)(swap.start)
    pooled = pooled + add_half(core)

    @pl.when(z >= DIRECT)
    def _():
        swap.wait_recv()

    @pl.when(z < DIRECT)
    def _():
        all_of(recv.at[0], d_recv.at[1]).wait()

    pooled = pooled + add_half(other)

    out = yz[W : 2 * W] + bias + pooled * scale
    o_ref[...] = jnp.maximum(out, 0.0).astype(BF)
    all_of(others, y_send).wait()
    all_of(rest, d_send.at[0]).wait()
    all_of(recv.at[0, pl.ds(0, NX * DIRECT)], d_send.at[1]).wait()

    @pl.when(z >= DIRECT)
    def _():
        swap.wait_send()


def shards(
    features, weight, bias, local_src, local_dst, hub_rows, hub_src, hub_dst, send_rows,
    bnd_src, bnd_dst,
):
    V = pltpu.VMEM
    I32 = jnp.int32
    DMA = pltpu.SemaphoreType.DMA
    REGULAR = pltpu.SemaphoreType.REGULAR
    out = pl.pallas_call(
        kernel,
        out_shape=jax.ShapeDtypeStruct((W, NODES), BF),
        in_specs=[pl.BlockSpec(memory_space=pl.ANY)] * 11,
        out_specs=pl.BlockSpec(memory_space=pltpu.VMEM),
        scratch_shapes=[
            V((W, NODES), BF), V((1, W), BF), V((16, 128), I32), V((16, 128), I32),
            V((1, 16), I32), V((16, 128), I32), V((16, 128), I32), V((8, 96), I32),
            V((NY, W, NODES), BF), V((NODES, 1024), BF),
            V((NODES, EDGES), BF), V((NODES + 16, EDGES), BF),
            V((NODES, EDGES // 2), BF), V((4 * HUBS + 16, EDGES // 2), BF),
            V((NODES, NODES), BF), V((8 * LINES, NODES), BF), V((ROWS, 256), BF),
            V((ROWS, LINES), BF), V((NQ, 8, 128), BF), V((2, NQ, 8, 128), BF),
            DMA((11,)), REGULAR, REGULAR, DMA(()), DMA(()), DMA((2,)), DMA((2,)),
            DMA(()), DMA(()),
        ],
        compiler_params=pltpu.CompilerParams(
            collective_id=0, has_side_effects=True, vmem_limit_bytes=56 * 1024 * 1024
        ),
    )(
        features.T, weight.T, bias.reshape(1, W),
        local_src.reshape(16, 128), local_dst.reshape(16, 128), hub_rows.reshape(1, 16),
        hub_src.reshape(8, 128), hub_dst.reshape(8, 128), send_rows.T,
        bnd_src.reshape(8, 128), bnd_dst.reshape(8, 128),
    )
    return out.T


def solution(mesh):
    return jax.shard_map(
        shards,
        mesh=mesh,
        in_specs=(
            P("dom", "feat"), P(None, "feat"), P("feat"), P("dom"), P("dom"), P("dom"),
            P("dom"), P("dom"), P("dom", None), P("dom"), P("dom"),
        ),
        out_specs=P("dom", "feat"),
        check_vma=False,
    )
```

```python
import jax
import jax.numpy as jnp
from jax import lax
from jax.experimental import pallas as pl
from jax.experimental.pallas import tpu as pltpu
from jax.sharding import PartitionSpec as P

MESH = pl.DeviceIdType.MESH
BF = jnp.bfloat16
F32 = jnp.float32
NX, NZ, NY = 4, 12, 8
NQ = NX * NZ
NODES = 512
W = 32
EDGES = 2048
ROWS = NQ * 8
HUBS = NQ * 4
BNDS = NQ * 2
LINES = HUBS + BNDS
EARLY = 6
Y_ORDER = (4, 3, 5, 2, 6, 1, 7)


def nt(a, b):
    return lax.dot_general(a, b, (((1,), (1,)), ((), ())), preferred_element_type=F32)


def nn(a, b):
    return jnp.dot(a, b, preferred_element_type=F32)


def one_hot(row, size):
    at = lax.broadcasted_iota(jnp.int32, (size, row.shape[1]), 0)
    return jnp.where(at == row, 1.0, 0.0).astype(BF)


def kernel(
    x_hbm, w_hbm, b_hbm, ls_hbm, ld_hbm, hr_hbm, hs_hbm, hd_hbm, sr_hbm, bs_hbm, bd_hbm,
    o_ref,
    w_v, b_v, ls_v, ld_v, hr_v, es_v, ed_v, sr_v, xg, ng, ot, ld1, ls1, ed1, es1, al, ar, pick, sel,
    sendb, recv, in_sem, ready, heard, all_in, y_send, y_recv, d_send, d_recv, c_send, c_recv,
):
    dom, f = lax.axis_index("dom"), lax.axis_index("feat")
    core = dom % 2
    q = dom // 2
    z, x = q % NZ, q // NZ

    def chip(xx, zz, on=core):
        return {"dom": (xx * NZ + zz) * 2 + on}

    other = 1 - core
    sibling = chip(x, z, other)

    def peer(i):
        return {"feat": lax.rem(f + i, NY)}

    def signal(sem, device_id):
        pl.semaphore_signal(sem, inc=1, device_id=device_id, device_id_type=MESH)

    loads = []
    for n, (src, dst) in enumerate((
        (x_hbm, xg.at[f]), (sr_hbm, sr_v), (hr_hbm, hr_v), (w_hbm, w_v), (b_hbm, b_v),
        (ls_hbm, ls_v), (ld_hbm, ld_v),
        (hs_hbm, es_v.at[pl.ds(0, 8)]), (bs_hbm, es_v.at[pl.ds(8, 8)]),
        (hd_hbm, ed_v.at[pl.ds(0, 8)]), (bd_hbm, ed_v.at[pl.ds(8, 8)]),
    )):
        copy = pltpu.make_async_copy(src, dst, in_sem.at[n])
        copy.start()
        loads.append(copy)

    rank = jnp.where(f <= NY // 2, jnp.maximum(2 * f - 1, 0), 2 * (NY - f))

    def at_rank(r):
        return {"feat": jnp.where(r % 2 == 1, (r + 1) // 2, lax.rem(NY - r // 2, NY))}

    barrier = pltpu.get_barrier_semaphore()

    @pl.loop(rank + 1, NY)
    def _(r):
        signal(barrier, at_rank(r))

    signal(barrier, sibling)
    for dx in range(1, NX):
        for on in range(2):
            signal(barrier, chip(lax.rem(x + dx, NX), z, on))

    @pl.when(z < EARLY)
    def _():
        @pl.loop(z + 1, NZ)
        def _(zz):
            for xx in range(NX):
                for on in range(2):
                    signal(barrier, chip(xx, zz, on))

    for copy in loads:
        copy.wait()

    lane = lax.broadcasted_iota(jnp.int32, (16, 512), 1)
    hub = lax.broadcasted_iota(jnp.int32, (16, 512), 0)
    spread = jnp.where(
        (lane // 128 == hub % 4) & (lane % 128 == 96 + hub // 4), 1.0, 0.0
    ).astype(BF)
    hub_lanes = nn(one_hot(hr_v[...], NODES), spread)
    for c in range(8):
        part = one_hot(sr_v[c : c + 1, :], NODES)
        part = jnp.concatenate([part, jnp.zeros((NODES, 32), BF)], axis=1)
        j, si = c % 4, c // 4
        if si == 0:
            part = part + hub_lanes[:, j * 128 : j * 128 + 128].astype(BF)
        ot[:, j * 256 + si * 128 : j * 256 + si * 128 + 128] = part
    row = lax.broadcasted_iota(jnp.int32, (ROWS, 256), 0)
    col = lax.broadcasted_iota(jnp.int32, (ROWS, 256), 1)
    t = row % 8
    want = jnp.where(t < 4, (t % 2) * 128 + (row // 8) * 2 + t // 2, 92 + t)
    pick[...] = jnp.where(col == want, 1.0, 0.0).astype(BF)
    line = lax.broadcasted_iota(jnp.int32, (ROWS, LINES), 0)
    at = lax.broadcasted_iota(jnp.int32, (ROWS, LINES), 1)
    low = at - HUBS
    want = jnp.where(low < 0, (at // 4) * 8 + 4 + at % 4, (low // 2) * 8 + 2 * core + low % 2)
    sel[...] = jnp.where(line == want, 1.0, 0.0).astype(BF)

    def all_of(region, sem):
        return pltpu.make_async_copy(region, region, sem)

    own = xg[f]
    lists = jnp.concatenate(
        [nn(own, ot[:, j * 256 : j * 256 + 256]) for j in range(4)], axis=0
    ).astype(BF)
    sendb[...] = nt(pick[...], lists).reshape(NQ, 8, 128).astype(BF)

    def send_rows_to(xx, zz):
        pltpu.make_async_remote_copy(
            src_ref=sendb.at[xx * NZ + zz], dst_ref=recv.at[core, q], send_sem=d_send.at[0],
            recv_sem=d_recv.at[0], device_id=chip(xx, zz), device_id_type=MESH,
        ).start()

    def send_across(xx, zz):
        pltpu.make_async_remote_copy(
            src_ref=sendb.at[xx * NZ + zz], dst_ref=recv.at[core, q], send_sem=d_send.at[1],
            recv_sem=d_recv.at[1], device_id=chip(xx, zz, other), device_id_type=MESH,
        ).start()

    def send_plane(zz):
        for dx in range(1, NX):
            send_rows_to(lax.rem(x + dx, NX), zz)

        @pl.when(zz != z)
        def _():
            send_rows_to(x, zz)

    def send_early_plane(zz):
        send_plane(zz)
        for xx in range(NX):
            send_across(xx, zz)

    pl.semaphore_wait(barrier, rank + 2 * NX - 1 + 2 * NX * jnp.minimum(z, EARLY))

    @pl.when(z > 0)
    def _():
        for xx in range(NX):
            signal(heard, chip(xx, 0))

    pl.loop(0, jnp.minimum(z + 1, EARLY))(send_early_plane)

    @pl.when(z >= EARLY)
    def _():
        for dx in range(1, NX):
            send_rows_to(lax.rem(x + dx, NX), z)

    @pl.loop(0, rank)
    def _(r):
        signal(ready, at_rank(r))

    recv[core, q] = sendb[q]

    def hot_rows(ref, at, out, size, first=0):
        @pl.loop(0, out.shape[1] // 128)
        def _(i):
            lanes = pl.ds(pl.multiple_of(i * 128, 128), 128)
            out[0:size, lanes] = one_hot(ref[pl.ds(first + i, 1), :] - at, size)

    ls1[NODES : NODES + 16, :] = jnp.ones((16, EDGES), BF)
    es1[4 * HUBS : 4 * HUBS + 16, :] = jnp.ones((16, EDGES // 2), BF)
    hot_rows(ls_v, 0, ls1, NODES)
    hot_rows(ld_v, 0, ld1, NODES)
    counts = nt(ls1[...], ld1[...])
    al[...] = counts[:NODES].astype(BF)
    degree = counts[NODES : NODES + 1]

    def to_peers(block, n):
        for i in Y_ORDER:
            pltpu.make_async_remote_copy(
                src_ref=block.at[f], dst_ref=block.at[f], send_sem=y_send.at[n],
                recv_sem=y_recv.at[n], device_id=peer(i), device_id_type=MESH,
            ).start()

    others = xg.at[pl.ds(0, NY - 1)]

    @pl.when(rank < NY - 1)
    def _():
        pl.semaphore_wait(ready, NY - 1 - rank)

    to_peers(xg, 0)

    h = es_v[0:8, :]
    s = h // 16
    es_v[0:8, :] = (s % 2) * (4 * HUBS) + (h % 4) * HUBS + (s // 2) * 4 + (h // 4) % 4
    b = es_v[8:16, :]
    s = b // 8
    es_v[8:16, :] = (s % 2) * (4 * BNDS) + (b % 4) * BNDS + (s // 2) * 2 + (b // 4) % 2

    hot_rows(ed_v, 0, ed1, NODES)
    for side in range(2):
        hot_rows(es_v, side * (4 * HUBS), es1, 4 * HUBS)
        got = nt(es1[...], ed1[...])
        for j in range(4):
            base = (side * 4 + j) * LINES
            ar[base : base + HUBS, :] = got[j * HUBS : (j + 1) * HUBS].astype(BF)
    degree = degree + got[4 * HUBS : 4 * HUBS + 1]
    @pl.when(z == 0)
    def _():
        pl.semaphore_wait(heard, NX * (NZ - 1))

        @pl.when(x > 0)
        def _():
            @pl.loop(0, NZ - 1)
            def _(i):
                zz = lax.rem(i + 5, NZ - 1) + 1
                signal(all_in, chip(x, zz))

                @pl.when(x == 1)
                def _():
                    signal(all_in, chip(0, zz))

    @pl.when(z > 0)
    def _():
        pl.semaphore_wait(all_in, 1)

    pl.loop(jnp.minimum(z + 1, EARLY), EARLY)(send_early_plane)

    @pl.loop(EARLY, NZ)
    def _(zz):
        @pl.when(zz != z)
        def _():
            for xx in range(NX):
                send_rows_to(xx, zz)

    hot_rows(ed_v, 0, ed1, NODES, 8)
    for side in range(2):
        hot_rows(es_v, side * (4 * BNDS), es1, 4 * BNDS, 8)
        got = nt(es1[0 : 4 * BNDS, :], ed1[...])
        for j in range(4):
            base = (side * 4 + j) * LINES + HUBS
            ar[base : base + BNDS, :] = got[j * BNDS : (j + 1) * BNDS].astype(BF)
    degree = degree + nt(es1[4 * HUBS : 4 * HUBS + 16, :], ed1[...])[0:1]
    scale = 1.0 / jnp.maximum(degree, 1.0)
    diag = lax.broadcasted_iota(jnp.int32, (W, W), 0) == lax.broadcasted_iota(jnp.int32, (W, W), 1)
    bias = jnp.sum(jnp.where(diag, b_v[...].astype(F32), 0.0), axis=1, keepdims=True)
    eye = jnp.where(
        lax.broadcasted_iota(jnp.int32, (128, 128), 0)
        == lax.broadcasted_iota(jnp.int32, (128, 128), 1), 1.0, 0.0,
    ).astype(BF)

    pooled = nn(own, al[...])
    all_of(others, y_recv.at[0]).wait()
    own_term = nn(w_v[:, 0:256], xg[...].reshape(NY * W, NODES)) + bias

    def add_half(side):
        rows = recv[side].reshape(ROWS, 128)
        turned = nn(nt(eye, rows).astype(BF), sel[...]).astype(BF)
        wide = jnp.concatenate([turned[j * W : j * W + W] for j in range(4)], axis=1)
        return nn(wide, ar[pl.ds(pl.multiple_of(side * (4 * LINES), 16), 4 * LINES), :])

    rest = recv.at[0, pl.ds(0, NQ - 1)]
    all_of(rest, d_recv.at[0]).wait()
    swap = pltpu.make_async_remote_copy(
        src_ref=recv.at[core], dst_ref=recv.at[core], send_sem=c_send, recv_sem=c_recv,
        device_id=sibling, device_id_type=MESH,
    )
    pl.when(z >= EARLY)(swap.start)
    pooled = pooled + add_half(core)

    @pl.when(z >= EARLY)
    def _():
        swap.wait_recv()

    @pl.when(z < EARLY)
    def _():
        all_of(recv.at[0], d_recv.at[1]).wait()

    pooled = pooled + add_half(other)

    ng[f] = (pooled * scale).astype(BF)
    to_peers(ng, 1)
    all_of(others, y_recv.at[1]).wait()
    out = own_term + nn(w_v[:, 256:512], ng[...].reshape(NY * W, NODES))
    o_ref[...] = jnp.maximum(out, 0.0).astype(BF)
    all_of(others, y_send.at[0]).wait()
    all_of(others, y_send.at[1]).wait()
    all_of(rest, d_send.at[0]).wait()
    all_of(recv.at[0, pl.ds(0, NX * EARLY)], d_send.at[1]).wait()

    @pl.when(z >= EARLY)
    def _():
        swap.wait_send()


def shards(
    features, weight, bias, local_src, local_dst, hub_rows, hub_src, hub_dst, send_rows,
    bnd_src, bnd_dst,
):
    V = pltpu.VMEM
    I32 = jnp.int32
    DMA = pltpu.SemaphoreType.DMA
    REGULAR = pltpu.SemaphoreType.REGULAR
    out = pl.pallas_call(
        kernel,
        out_shape=jax.ShapeDtypeStruct((W, NODES), BF),
        in_specs=[pl.BlockSpec(memory_space=pl.ANY)] * 11,
        out_specs=pl.BlockSpec(memory_space=pltpu.VMEM),
        scratch_shapes=[
            V((W, NODES), BF), V((1, W), BF), V((16, 128), I32), V((16, 128), I32),
            V((1, 16), I32), V((16, 128), I32), V((16, 128), I32), V((8, 96), I32),
            V((NY, W, NODES), BF), V((NY, W, NODES), BF), V((NODES, 1024), BF),
            V((NODES, EDGES), BF), V((NODES + 16, EDGES), BF),
            V((NODES, EDGES // 2), BF), V((4 * HUBS + 16, EDGES // 2), BF),
            V((NODES, NODES), BF), V((8 * LINES, NODES), BF), V((ROWS, 256), BF),
            V((ROWS, LINES), BF), V((NQ, 8, 128), BF), V((2, NQ, 8, 128), BF),
            DMA((11,)), REGULAR, REGULAR, REGULAR, DMA((2,)), DMA((2,)), DMA((2,)), DMA((2,)),
            DMA(()), DMA(()),
        ],
        compiler_params=pltpu.CompilerParams(
            collective_id=0, has_side_effects=True, vmem_limit_bytes=56 * 1024 * 1024
        ),
    )(
        features.T, weight.T, bias.reshape(1, W),
        local_src.reshape(16, 128), local_dst.reshape(16, 128), hub_rows.reshape(1, 16),
        hub_src.reshape(8, 128), hub_dst.reshape(8, 128), send_rows.T,
        bnd_src.reshape(8, 128), bnd_dst.reshape(8, 128),
    )
    return out.T


def solution(mesh):
    return jax.shard_map(
        shards,
        mesh=mesh,
        in_specs=(
            P("dom", "feat"), P(None, "feat"), P("feat"), P("dom"), P("dom"), P("dom"),
            P("dom"), P("dom"), P("dom", None), P("dom"), P("dom"),
        ),
        out_specs=P("dom", "feat"),
        check_vma=False,
    )
```

```python
import jax
import jax.numpy as jnp
from jax import lax
from jax.experimental import pallas as pl
from jax.experimental.pallas import tpu as pltpu
from jax.sharding import PartitionSpec as P

MESH = pl.DeviceIdType.MESH
BF = jnp.bfloat16
F32 = jnp.float32
NX, NZ, NY = 4, 12, 8
NQ = NX * NZ
NODES = 512
W = 32
EDGES = 2048
ROWS = NQ * 8
HUBS = NQ * 4
BNDS = NQ * 2
LINES = HUBS + BNDS
EARLY = 6
DIRECT = 3
Y_ORDER = (4, 5, 3, 6, 2, 7, 1)


def nt(a, b):
    return lax.dot_general(a, b, (((1,), (1,)), ((), ())), preferred_element_type=F32)


def nn(a, b):
    return jnp.dot(a, b, preferred_element_type=F32)


def one_hot(row, size):
    at = lax.broadcasted_iota(jnp.int32, (size, row.shape[1]), 0)
    return jnp.where(at == row, 1.0, 0.0).astype(BF)


def kernel(
    x_hbm, w_hbm, b_hbm, ls_hbm, ld_hbm, hr_hbm, hs_hbm, hd_hbm, sr_hbm, bs_hbm, bd_hbm,
    o_ref,
    w_v, b_v, ls_v, ld_v, hr_v, es_v, ed_v, sr_v, xg, ng, ot, ld1, ls1, ed1, es1, al, ar, pick, sel,
    sendb, recv, in_sem, ready, heard, all_in, y_send, y_recv, d_send, d_recv, c_send, c_recv,
):
    dom, f = lax.axis_index("dom"), lax.axis_index("feat")
    core = dom % 2
    q = dom // 2
    z, x = q % NZ, q // NZ

    def chip(xx, zz, on=core):
        return {"dom": (xx * NZ + zz) * 2 + on}

    other = 1 - core
    sibling = chip(x, z, other)

    def peer(i):
        return {"feat": lax.rem(f + i, NY)}

    def signal(sem, device_id):
        pl.semaphore_signal(sem, inc=1, device_id=device_id, device_id_type=MESH)

    loads = []
    for n, (src, dst) in enumerate((
        (x_hbm, xg.at[f]), (sr_hbm, sr_v), (hr_hbm, hr_v), (w_hbm, w_v), (b_hbm, b_v),
        (ls_hbm, ls_v), (ld_hbm, ld_v),
        (hs_hbm, es_v.at[pl.ds(0, 8)]), (bs_hbm, es_v.at[pl.ds(8, 8)]),
        (hd_hbm, ed_v.at[pl.ds(0, 8)]), (bd_hbm, ed_v.at[pl.ds(8, 8)]),
    )):
        copy = pltpu.make_async_copy(src, dst, in_sem.at[n])
        copy.start()
        loads.append(copy)

    rank = jnp.where(f <= NY // 2, jnp.maximum(2 * f - 1, 0), 2 * (NY - f))

    def at_rank(r):
        return {"feat": jnp.where(r % 2 == 1, (r + 1) // 2, lax.rem(NY - r // 2, NY))}

    barrier = pltpu.get_barrier_semaphore()

    @pl.loop(rank + 1, NY)
    def _(r):
        signal(barrier, at_rank(r))

    signal(barrier, sibling)
    for dx in range(1, NX):
        for on in range(2):
            signal(barrier, chip(lax.rem(x + dx, NX), z, on))

    @pl.when(z < EARLY)
    def _():
        @pl.loop(z + 1, NZ)
        def _(zz):
            for xx in range(NX):
                for on in range(2):
                    signal(barrier, chip(xx, zz, on))

    lane = lax.broadcasted_iota(jnp.int32, (16, 512), 1)
    hub = lax.broadcasted_iota(jnp.int32, (16, 512), 0)
    spread = jnp.where(
        (lane // 128 == hub % 4) & (lane % 128 == 96 + hub // 4), 1.0, 0.0
    ).astype(BF)
    row = lax.broadcasted_iota(jnp.int32, (ROWS, 256), 0)
    col = lax.broadcasted_iota(jnp.int32, (ROWS, 256), 1)
    t = row % 8
    want = jnp.where(t < 4, (t % 2) * 128 + (row // 8) * 2 + t // 2, 92 + t)
    pick[...] = jnp.where(col == want, 1.0, 0.0).astype(BF)
    for copy in loads[:3]:
        copy.wait()

    hub_lanes = nn(one_hot(hr_v[...], NODES), spread)
    for c in range(8):
        part = one_hot(sr_v[c : c + 1, :], NODES)
        part = jnp.concatenate([part, jnp.zeros((NODES, 32), BF)], axis=1)
        j, si = c % 4, c // 4
        if si == 0:
            part = part + hub_lanes[:, j * 128 : j * 128 + 128].astype(BF)
        ot[:, j * 256 + si * 128 : j * 256 + si * 128 + 128] = part

    pl.semaphore_wait(barrier, rank + 2 * NX - 1 + 2 * NX * jnp.minimum(z, EARLY))

    @pl.when(z > 0)
    def _():
        for xx in range(NX):
            signal(heard.at[z], chip(xx, 0))

    def all_of(region, sem):
        return pltpu.make_async_copy(region, region, sem)

    own = xg[f]
    lists = jnp.concatenate(
        [nn(own, ot[:, j * 256 : j * 256 + 256]) for j in range(4)], axis=0
    ).astype(BF)
    sendb[...] = nt(pick[...], lists).reshape(NQ, 8, 128).astype(BF)

    def send_rows_to(xx, zz):
        pltpu.make_async_remote_copy(
            src_ref=sendb.at[xx * NZ + zz], dst_ref=recv.at[core, q], send_sem=d_send.at[0],
            recv_sem=d_recv.at[0], device_id=chip(xx, zz), device_id_type=MESH,
        ).start()

    def send_across(xx, zz):
        pltpu.make_async_remote_copy(
            src_ref=sendb.at[xx * NZ + zz], dst_ref=recv.at[core, q], send_sem=d_send.at[1],
            recv_sem=d_recv.at[1], device_id=chip(xx, zz, other), device_id_type=MESH,
        ).start()

    def send_plane(zz):
        for dx in range(1, NX):
            send_rows_to(lax.rem(x + dx, NX), zz)

        @pl.when(zz != z)
        def _():
            send_rows_to(x, zz)

    def send_early_plane(zz):
        send_plane(zz)

        @pl.when(zz < DIRECT)
        def _():
            for xx in range(NX):
                send_across(xx, zz)

    pl.loop(0, jnp.minimum(z + 1, EARLY))(send_early_plane)

    @pl.when(z >= EARLY)
    def _():
        for dx in range(1, NX):
            send_rows_to(lax.rem(x + dx, NX), z)

    @pl.loop(0, rank)
    def _(r):
        signal(ready, at_rank(r))

    recv[core, q] = sendb[q]
    for copy in loads[3:]:
        copy.wait()

    def hot_rows(ref, at, out, size, first=0):
        @pl.loop(0, out.shape[1] // 128)
        def _(i):
            lanes = pl.ds(pl.multiple_of(i * 128, 128), 128)
            out[0:size, lanes] = one_hot(ref[pl.ds(first + i, 1), :] - at, size)

    ls1[NODES : NODES + 16, :] = jnp.ones((16, EDGES), BF)
    es1[4 * HUBS : 4 * HUBS + 16, :] = jnp.ones((16, EDGES // 2), BF)
    hot_rows(ls_v, 0, ls1, NODES)
    hot_rows(ld_v, 0, ld1, NODES)
    counts = nt(ls1[...], ld1[...])
    al[...] = counts[:NODES].astype(BF)
    degree = counts[NODES : NODES + 1]

    def to_peers(block, n):
        for i in Y_ORDER:
            pltpu.make_async_remote_copy(
                src_ref=block.at[f], dst_ref=block.at[f], send_sem=y_send.at[n],
                recv_sem=y_recv.at[n], device_id=peer(i), device_id_type=MESH,
            ).start()

    others = xg.at[pl.ds(0, NY - 1)]

    @pl.when(rank < NY - 1)
    def _():
        pl.semaphore_wait(ready, NY - 1 - rank)

    to_peers(xg, 0)

    def send_late_plane(zz):
        for xx in range(NX):
            send_rows_to(xx, zz)

    @pl.when(z >= EARLY)
    def _():
        pl.semaphore_wait(all_in, 1)
        pl.loop(EARLY, z)(send_late_plane)
        pl.loop(z + 1, NZ)(send_late_plane)

    line = lax.broadcasted_iota(jnp.int32, (ROWS, LINES), 0)
    at = lax.broadcasted_iota(jnp.int32, (ROWS, LINES), 1)
    low = at - HUBS
    want = jnp.where(low < 0, (at // 4) * 8 + 4 + at % 4, (low // 2) * 8 + 2 * core + low % 2)
    sel[...] = jnp.where(line == want, 1.0, 0.0).astype(BF)

    h = es_v[0:8, :]
    s = h // 16
    es_v[0:8, :] = (s % 2) * (4 * HUBS) + (h % 4) * HUBS + (s // 2) * 4 + (h // 4) % 4
    b = es_v[8:16, :]
    s = b // 8
    es_v[8:16, :] = (s % 2) * (4 * BNDS) + (b % 4) * BNDS + (s // 2) * 2 + (b // 4) % 2

    hot_rows(ed_v, 0, ed1, NODES)
    for side in range(2):
        hot_rows(es_v, side * (4 * HUBS), es1, 4 * HUBS)
        got = nt(es1[...], ed1[...])
        for j in range(4):
            base = (side * 4 + j) * LINES
            ar[base : base + HUBS, :] = got[j * HUBS : (j + 1) * HUBS].astype(BF)
    degree = degree + got[4 * HUBS : 4 * HUBS + 1]
    @pl.when(z == 0)
    def _():
        @pl.loop(1, NZ)
        def _(zz):
            pl.semaphore_wait(heard.at[zz], NX)

            @pl.when(zz < EARLY)
            def _():
                send_early_plane(zz)

            @pl.when(zz >= EARLY)
            def _():
                send_late_plane(zz)

        @pl.when(x > 0)
        def _():
            @pl.loop(0, NZ - 1)
            def _(i):
                zz = lax.rem(i + 5, NZ - 1) + 1
                signal(all_in, chip(x, zz))

                @pl.when(x == 1)
                def _():
                    signal(all_in, chip(0, zz))

    hot_rows(ed_v, 0, ed1, NODES, 8)
    for side in range(2):
        hot_rows(es_v, side * (4 * BNDS), es1, 4 * BNDS, 8)
        got = nt(es1[0 : 4 * BNDS, :], ed1[...])
        for j in range(4):
            base = (side * 4 + j) * LINES + HUBS
            ar[base : base + BNDS, :] = got[j * BNDS : (j + 1) * BNDS].astype(BF)
    degree = degree + nt(es1[4 * HUBS : 4 * HUBS + 16, :], ed1[...])[0:1]
    scale = 1.0 / jnp.maximum(degree, 1.0)

    @pl.when((z > 0) & (z < EARLY))
    def _():
        pl.semaphore_wait(all_in, 1)
        pl.loop(z + 1, EARLY)(send_early_plane)
        pl.loop(EARLY, NZ)(send_late_plane)

    diag = lax.broadcasted_iota(jnp.int32, (W, W), 0) == lax.broadcasted_iota(jnp.int32, (W, W), 1)
    bias = jnp.sum(jnp.where(diag, b_v[...].astype(F32), 0.0), axis=1, keepdims=True)
    eye = jnp.where(
        lax.broadcasted_iota(jnp.int32, (128, 128), 0)
        == lax.broadcasted_iota(jnp.int32, (128, 128), 1), 1.0, 0.0,
    ).astype(BF)

    pooled = nn(own, al[...])
    all_of(others, y_recv.at[0]).wait()
    own_term = nn(w_v[:, 0:256], xg[...].reshape(NY * W, NODES)) + bias

    def add_half(side):
        rows = recv[side].reshape(ROWS, 128)
        turned = nn(nt(eye, rows).astype(BF), sel[...]).astype(BF)
        wide = jnp.concatenate([turned[j * W : j * W + W] for j in range(4)], axis=1)
        return nn(wide, ar[pl.ds(pl.multiple_of(side * (4 * LINES), 16), 4 * LINES), :])

    rest = recv.at[0, pl.ds(0, NQ - 1)]
    all_of(rest, d_recv.at[0]).wait()
    swap = pltpu.make_async_remote_copy(
        src_ref=recv.at[core], dst_ref=recv.at[core], send_sem=c_send, recv_sem=c_recv,
        device_id=sibling, device_id_type=MESH,
    )
    pl.when(z >= DIRECT)(swap.start)
    pooled = pooled + add_half(core)

    @pl.when(z >= DIRECT)
    def _():
        swap.wait_recv()

    @pl.when(z < DIRECT)
    def _():
        all_of(recv.at[0], d_recv.at[1]).wait()

    pooled = pooled + add_half(other)

    ng[f] = (pooled * scale).astype(BF)
    to_peers(ng, 1)
    all_of(others, y_recv.at[1]).wait()
    out = own_term + nn(w_v[:, 256:512], ng[...].reshape(NY * W, NODES))
    o_ref[...] = jnp.maximum(out, 0.0).astype(BF)
    all_of(others, y_send.at[0]).wait()
    all_of(others, y_send.at[1]).wait()
    all_of(rest, d_send.at[0]).wait()
    all_of(recv.at[0, pl.ds(0, NX * DIRECT)], d_send.at[1]).wait()

    @pl.when(z >= DIRECT)
    def _():
        swap.wait_send()


def shards(
    features, weight, bias, local_src, local_dst, hub_rows, hub_src, hub_dst, send_rows,
    bnd_src, bnd_dst,
):
    V = pltpu.VMEM
    I32 = jnp.int32
    DMA = pltpu.SemaphoreType.DMA
    REGULAR = pltpu.SemaphoreType.REGULAR
    out = pl.pallas_call(
        kernel,
        out_shape=jax.ShapeDtypeStruct((W, NODES), BF),
        in_specs=[pl.BlockSpec(memory_space=pl.ANY)] * 11,
        out_specs=pl.BlockSpec(memory_space=pltpu.VMEM),
        scratch_shapes=[
            V((W, NODES), BF), V((1, W), BF), V((16, 128), I32), V((16, 128), I32),
            V((1, 16), I32), V((16, 128), I32), V((16, 128), I32), V((8, 96), I32),
            V((NY, W, NODES), BF), V((NY, W, NODES), BF), V((NODES, 1024), BF),
            V((NODES, EDGES), BF), V((NODES + 16, EDGES), BF),
            V((NODES, EDGES // 2), BF), V((4 * HUBS + 16, EDGES // 2), BF),
            V((NODES, NODES), BF), V((8 * LINES, NODES), BF), V((ROWS, 256), BF),
            V((ROWS, LINES), BF), V((NQ, 8, 128), BF), V((2, NQ, 8, 128), BF),
            DMA((11,)), REGULAR, REGULAR((NZ,)), REGULAR, DMA((2,)), DMA((2,)), DMA((2,)), DMA((2,)),
            DMA(()), DMA(()),
        ],
        compiler_params=pltpu.CompilerParams(
            collective_id=0, has_side_effects=True, vmem_limit_bytes=56 * 1024 * 1024
        ),
    )(
        features.T, weight.T, bias.reshape(1, W),
        local_src.reshape(16, 128), local_dst.reshape(16, 128), hub_rows.reshape(1, 16),
        hub_src.reshape(8, 128), hub_dst.reshape(8, 128), send_rows.T,
        bnd_src.reshape(8, 128), bnd_dst.reshape(8, 128),
    )
    return out.T


def solution(mesh):
    return jax.shard_map(
        shards,
        mesh=mesh,
        in_specs=(
            P("dom", "feat"), P(None, "feat"), P("feat"), P("dom"), P("dom"), P("dom"),
            P("dom"), P("dom"), P("dom", None), P("dom"), P("dom"),
        ),
        out_specs=P("dom", "feat"),
        check_vma=False,
    )
```

```python
import jax
import jax.numpy as jnp
from jax import lax
from jax.experimental import pallas as pl
from jax.experimental.pallas import tpu as pltpu
from jax.sharding import PartitionSpec as P

MESH = pl.DeviceIdType.MESH
BF = jnp.bfloat16
F32 = jnp.float32
NX, NZ, NY = 4, 12, 8
NQ = NX * NZ
NODES = 512
W = 32
EDGES = 2048
ROWS = NQ * 8
HUBS = NQ * 4
BNDS = NQ * 2
LINES = HUBS + BNDS
EARLY = 6
DIRECT = 3
Y_ORDER = (4, 5, 3, 6, 2, 7, 1)


def nt(a, b):
    return lax.dot_general(a, b, (((1,), (1,)), ((), ())), preferred_element_type=F32)


def nn(a, b):
    return jnp.dot(a, b, preferred_element_type=F32)


def one_hot(row, size):
    at = lax.broadcasted_iota(jnp.int32, (size, row.shape[1]), 0)
    return jnp.where(at == row, 1.0, 0.0).astype(BF)


def kernel(
    x_hbm, w_hbm, b_hbm, ls_hbm, ld_hbm, hr_hbm, hs_hbm, hd_hbm, sr_hbm, bs_hbm, bd_hbm,
    o_ref,
    w_v, b_v, ls_v, ld_v, hr_v, es_v, ed_v, sr_v, xg, ng, ot, ld1, ls1, ed1, es1, al, ar, pick, sel,
    sendb, recv, in_sem, ready, heard, all_in, y_send, y_recv, d_send, d_recv, c_send, c_recv,
):
    dom, f = lax.axis_index("dom"), lax.axis_index("feat")
    core = dom % 2
    q = dom // 2
    z, x = q % NZ, q // NZ

    def chip(xx, zz, on=core):
        return {"dom": (xx * NZ + zz) * 2 + on}

    other = 1 - core
    sibling = chip(x, z, other)

    def peer(i):
        return {"feat": lax.rem(f + i, NY)}

    def signal(sem, device_id):
        pl.semaphore_signal(sem, inc=1, device_id=device_id, device_id_type=MESH)

    loads = []
    for n, (src, dst) in enumerate((
        (x_hbm, xg.at[f]), (sr_hbm, sr_v), (hr_hbm, hr_v), (w_hbm, w_v), (b_hbm, b_v),
        (ls_hbm, ls_v), (ld_hbm, ld_v),
        (hs_hbm, es_v.at[pl.ds(0, 8)]), (bs_hbm, es_v.at[pl.ds(8, 8)]),
        (hd_hbm, ed_v.at[pl.ds(0, 8)]), (bd_hbm, ed_v.at[pl.ds(8, 8)]),
    )):
        copy = pltpu.make_async_copy(src, dst, in_sem.at[n])
        copy.start()
        loads.append(copy)

    rank = jnp.where(f <= NY // 2, jnp.maximum(2 * f - 1, 0), 2 * (NY - f))

    def at_rank(r):
        return {"feat": jnp.where(r % 2 == 1, (r + 1) // 2, lax.rem(NY - r // 2, NY))}

    barrier = pltpu.get_barrier_semaphore()

    @pl.loop(rank + 1, NY)
    def _(r):
        signal(barrier, at_rank(r))

    signal(barrier, sibling)
    for dx in range(1, NX):
        for on in range(2):
            signal(barrier, chip(lax.rem(x + dx, NX), z, on))

    @pl.when(z < EARLY)
    def _():
        @pl.loop(z + 1, NZ)
        def _(zz):
            for xx in range(NX):
                for on in range(2):
                    signal(barrier, chip(xx, zz, on))

    lane = lax.broadcasted_iota(jnp.int32, (16, 512), 1)
    hub = lax.broadcasted_iota(jnp.int32, (16, 512), 0)
    spread = jnp.where(
        (lane // 128 == hub % 4) & (lane % 128 == 96 + hub // 4), 1.0, 0.0
    ).astype(BF)
    row = lax.broadcasted_iota(jnp.int32, (ROWS, 256), 0)
    col = lax.broadcasted_iota(jnp.int32, (ROWS, 256), 1)
    t = row % 8
    want = jnp.where(t < 4, (t % 2) * 128 + (row // 8) * 2 + t // 2, 92 + t)
    pick[...] = jnp.where(col == want, 1.0, 0.0).astype(BF)
    for copy in loads[:3]:
        copy.wait()

    hub_lanes = nn(one_hot(hr_v[...], NODES), spread)
    for c in range(8):
        part = one_hot(sr_v[c : c + 1, :], NODES)
        part = jnp.concatenate([part, jnp.zeros((NODES, 32), BF)], axis=1)
        j, si = c % 4, c // 4
        if si == 0:
            part = part + hub_lanes[:, j * 128 : j * 128 + 128].astype(BF)
        ot[:, j * 256 + si * 128 : j * 256 + si * 128 + 128] = part

    pl.semaphore_wait(barrier, rank + 2 * NX - 1 + 2 * NX * jnp.minimum(z, EARLY))

    @pl.when(z > 0)
    def _():
        for xx in range(NX):
            signal(heard.at[z], chip(xx, 0))

    def all_of(region, sem):
        return pltpu.make_async_copy(region, region, sem)

    own = xg[f]
    lists = jnp.concatenate(
        [nn(own, ot[:, j * 256 : j * 256 + 256]) for j in range(4)], axis=0
    ).astype(BF)
    sendb[...] = nt(pick[...], lists).reshape(NQ, 8, 128).astype(BF)

    def send_rows_to(xx, zz):
        pltpu.make_async_remote_copy(
            src_ref=sendb.at[xx * NZ + zz], dst_ref=recv.at[core, q], send_sem=d_send.at[0],
            recv_sem=d_recv.at[0], device_id=chip(xx, zz), device_id_type=MESH,
        ).start()

    def send_across(xx, zz):
        pltpu.make_async_remote_copy(
            src_ref=sendb.at[xx * NZ + zz], dst_ref=recv.at[core, q], send_sem=d_send.at[1],
            recv_sem=d_recv.at[1], device_id=chip(xx, zz, other), device_id_type=MESH,
        ).start()

    def send_plane(zz):
        for dx in range(1, NX):
            send_rows_to(lax.rem(x + dx, NX), zz)

        @pl.when(zz != z)
        def _():
            send_rows_to(x, zz)

    def send_early_plane(zz):
        send_plane(zz)

        @pl.when(zz < DIRECT)
        def _():
            for xx in range(NX):
                send_across(xx, zz)

    pl.loop(0, jnp.minimum(z + 1, EARLY))(send_early_plane)

    @pl.when(z >= EARLY)
    def _():
        for dx in range(1, NX):
            send_rows_to(lax.rem(x + dx, NX), z)

    @pl.loop(0, rank)
    def _(r):
        signal(ready, at_rank(r))

    recv[core, q] = sendb[q]
    for copy in loads[3:]:
        copy.wait()

    def hot_rows(ref, at, out, size, first=0):
        @pl.loop(0, out.shape[1] // 128)
        def _(i):
            lanes = pl.ds(pl.multiple_of(i * 128, 128), 128)
            out[0:size, lanes] = one_hot(ref[pl.ds(first + i, 1), :] - at, size)

    ls1[NODES : NODES + 16, :] = jnp.ones((16, EDGES), BF)
    es1[4 * HUBS : 4 * HUBS + 16, :] = jnp.ones((16, EDGES // 2), BF)
    hot_rows(ls_v, 0, ls1, NODES)
    hot_rows(ld_v, 0, ld1, NODES)
    counts = nt(ls1[...], ld1[...])
    al[...] = counts[:NODES].astype(BF)
    degree = counts[NODES : NODES + 1]

    def to_peers(block, n):
        for i in Y_ORDER:
            pltpu.make_async_remote_copy(
                src_ref=block.at[f], dst_ref=block.at[f], send_sem=y_send.at[n],
                recv_sem=y_recv.at[n], device_id=peer(i), device_id_type=MESH,
            ).start()

    others = xg.at[pl.ds(0, NY - 1)]

    @pl.when(rank < NY - 1)
    def _():
        pl.semaphore_wait(ready, NY - 1 - rank)

    to_peers(xg, 0)

    def send_late_plane(zz):
        for xx in range(NX):
            send_rows_to(xx, zz)

    @pl.when(z >= EARLY)
    def _():
        pl.semaphore_wait(all_in, 1)
        pl.loop(EARLY, z)(send_late_plane)
        pl.loop(z + 1, NZ)(send_late_plane)

    line = lax.broadcasted_iota(jnp.int32, (ROWS, LINES), 0)
    at = lax.broadcasted_iota(jnp.int32, (ROWS, LINES), 1)
    low = at - HUBS
    want = jnp.where(low < 0, (at // 4) * 8 + 4 + at % 4, (low // 2) * 8 + 2 * core + low % 2)
    sel[...] = jnp.where(line == want, 1.0, 0.0).astype(BF)

    h = es_v[0:8, :]
    s = h // 16
    es_v[0:8, :] = (s % 2) * (4 * HUBS) + (h % 4) * HUBS + (s // 2) * 4 + (h // 4) % 4
    b = es_v[8:16, :]
    s = b // 8
    es_v[8:16, :] = (s % 2) * (4 * BNDS) + (b % 4) * BNDS + (s // 2) * 2 + (b // 4) % 2

    hot_rows(ed_v, 0, ed1, NODES)
    for side in range(2):
        hot_rows(es_v, side * (4 * HUBS), es1, 4 * HUBS)
        got = nt(es1[...], ed1[...])
        for j in range(4):
            base = (side * 4 + j) * LINES
            ar[base : base + HUBS, :] = got[j * HUBS : (j + 1) * HUBS].astype(BF)
    degree = degree + got[4 * HUBS : 4 * HUBS + 1]
    @pl.when(z == 0)
    def _():
        @pl.loop(1, NZ)
        def _(zz):
            pl.semaphore_wait(heard.at[zz], NX)

            @pl.when(zz < EARLY)
            def _():
                send_early_plane(zz)

            @pl.when(zz >= EARLY)
            def _():
                send_late_plane(zz)

        @pl.when(x > 0)
        def _():
            @pl.loop(0, NZ - 1)
            def _(i):
                zz = lax.rem(i + 5, NZ - 1) + 1
                signal(all_in, chip(x, zz))

                @pl.when(x == 1)
                def _():
                    signal(all_in, chip(0, zz))

    hot_rows(ed_v, 0, ed1, NODES, 8)
    for side in range(2):
        hot_rows(es_v, side * (4 * BNDS), es1, 4 * BNDS, 8)
        got = nt(es1[0 : 4 * BNDS, :], ed1[...])
        for j in range(4):
            base = (side * 4 + j) * LINES + HUBS
            ar[base : base + BNDS, :] = got[j * BNDS : (j + 1) * BNDS].astype(BF)
    degree = degree + nt(es1[4 * HUBS : 4 * HUBS + 16, :], ed1[...])[0:1]
    scale = 1.0 / jnp.maximum(degree, 1.0)

    @pl.when((z > 0) & (z < EARLY))
    def _():
        pl.semaphore_wait(all_in, 1)
        pl.loop(z + 1, EARLY)(send_early_plane)
        pl.loop(EARLY, NZ)(send_late_plane)

    diag = lax.broadcasted_iota(jnp.int32, (W, W), 0) == lax.broadcasted_iota(jnp.int32, (W, W), 1)
    bias = jnp.sum(jnp.where(diag, b_v[...].astype(F32), 0.0), axis=1, keepdims=True)

    pooled = nn(own, al[...])
    all_of(others, y_recv.at[0]).wait()
    own_term = nn(w_v[:, 0:256], xg[...].reshape(NY * W, NODES)) + bias

    def add_half(side):
        rows = recv[side].reshape(ROWS, 128)
        turned = lax.dot_general(
            rows, sel[...], (((0,), (0,)), ((), ())), preferred_element_type=F32
        ).astype(BF)
        wide = jnp.concatenate([turned[j * W : j * W + W] for j in range(4)], axis=1)
        return nn(wide, ar[pl.ds(pl.multiple_of(side * (4 * LINES), 16), 4 * LINES), :])

    rest = recv.at[0, pl.ds(0, NQ - 1)]
    all_of(rest, d_recv.at[0]).wait()
    swap = pltpu.make_async_remote_copy(
        src_ref=recv.at[core], dst_ref=recv.at[core], send_sem=c_send, recv_sem=c_recv,
        device_id=sibling, device_id_type=MESH,
    )
    pl.when(z >= DIRECT)(swap.start)
    pooled = pooled + add_half(core)

    @pl.when(z >= DIRECT)
    def _():
        swap.wait_recv()

    @pl.when(z < DIRECT)
    def _():
        all_of(recv.at[0], d_recv.at[1]).wait()

    pooled = pooled + add_half(other)

    ng[f] = (pooled * scale).astype(BF)
    to_peers(ng, 1)
    all_of(others, y_recv.at[1]).wait()
    out = own_term + nn(w_v[:, 256:512], ng[...].reshape(NY * W, NODES))
    o_ref[...] = jnp.maximum(out, 0.0).astype(BF)
    all_of(others, y_send.at[0]).wait()
    all_of(others, y_send.at[1]).wait()
    all_of(rest, d_send.at[0]).wait()
    all_of(recv.at[0, pl.ds(0, NX * DIRECT)], d_send.at[1]).wait()

    @pl.when(z >= DIRECT)
    def _():
        swap.wait_send()


def shards(
    features, weight, bias, local_src, local_dst, hub_rows, hub_src, hub_dst, send_rows,
    bnd_src, bnd_dst,
):
    V = pltpu.VMEM
    I32 = jnp.int32
    DMA = pltpu.SemaphoreType.DMA
    REGULAR = pltpu.SemaphoreType.REGULAR
    out = pl.pallas_call(
        kernel,
        out_shape=jax.ShapeDtypeStruct((W, NODES), BF),
        in_specs=[pl.BlockSpec(memory_space=pl.ANY)] * 11,
        out_specs=pl.BlockSpec(memory_space=pltpu.VMEM),
        scratch_shapes=[
            V((W, NODES), BF), V((1, W), BF), V((16, 128), I32), V((16, 128), I32),
            V((1, 16), I32), V((16, 128), I32), V((16, 128), I32), V((8, 96), I32),
            V((NY, W, NODES), BF), V((NY, W, NODES), BF), V((NODES, 1024), BF),
            V((NODES, EDGES), BF), V((NODES + 16, EDGES), BF),
            V((NODES, EDGES // 2), BF), V((4 * HUBS + 16, EDGES // 2), BF),
            V((NODES, NODES), BF), V((8 * LINES, NODES), BF), V((ROWS, 256), BF),
            V((ROWS, LINES), BF), V((NQ, 8, 128), BF), V((2, NQ, 8, 128), BF),
            DMA((11,)), REGULAR, REGULAR((NZ,)), REGULAR, DMA((2,)), DMA((2,)), DMA((2,)), DMA((2,)),
            DMA(()), DMA(()),
        ],
        compiler_params=pltpu.CompilerParams(
            collective_id=0, has_side_effects=True, vmem_limit_bytes=56 * 1024 * 1024
        ),
    )(
        features.T, weight.T, bias.reshape(1, W),
        local_src.reshape(16, 128), local_dst.reshape(16, 128), hub_rows.reshape(1, 16),
        hub_src.reshape(8, 128), hub_dst.reshape(8, 128), send_rows.T,
        bnd_src.reshape(8, 128), bnd_dst.reshape(8, 128),
    )
    return out.T


def solution(mesh):
    return jax.shard_map(
        shards,
        mesh=mesh,
        in_specs=(
            P("dom", "feat"), P(None, "feat"), P("feat"), P("dom"), P("dom"), P("dom"),
            P("dom"), P("dom"), P("dom", None), P("dom"), P("dom"),
        ),
        out_specs=P("dom", "feat"),
        check_vma=False,
    )
```
